512 devices in a mesh: row: 64 (over x, z, core), col: 8 (over y).
Axes of the slice: x: 4, y: 8, z: 8, core: 2. Of those that a mesh axis runs over, the one named last changes fastest.
Arguments:
- image: float32 [16384, 768], P(('row', 'col')), may hold values from -4 to 4
- text: float32 [16384, 768], P(('col', 'row')), may hold values from -4 to 4
Outputs:
- loss: float32 [], replicated
- image_grad: float32 [16384, 768], P(('row', 'col'))
- text_grad: float32 [16384, 768], P(('col', 'row'))
The draws below stay inside these ranges and needn't reach their ends.
All inputs are finite; a program needn't handle non-finite values.
Results may differ from the reference program's by a relative error of at most 0.0003.
Values sent between devices are 32-bit elements; how exact they have to be, the bound alone decides.
A program may use at most 64 MiB of HBM per device.

```python
import math
import jax
import jax.numpy as jnp
from jax import lax

E = 768
BATCH = 16384


logit_spread = 3.0


def paired(key):
    key_base = jax.random.fold_in(key, 0)
    key_image = jax.random.fold_in(key, 1)
    key_text = jax.random.fold_in(key, 2)
    key_pick = jax.random.fold_in(key, 4)
    key_share = jax.random.fold_in(key, 5)
    shape = (BATCH, E)
    entry_scale = math.sqrt(logit_spread / (20.0 * math.sqrt(E)))
    base = jnp.clip(jax.random.normal(key_base, shape, jnp.float32), -4.0, 4.0)
    image_noise = jnp.clip(jax.random.normal(key_image, shape, jnp.float32), -4.0, 4.0)
    text_noise = jnp.clip(jax.random.normal(key_text, shape, jnp.float32), -4.0, 4.0)
    index = jnp.arange(BATCH)
    position = index.astype(jnp.float32) / BATCH
    share = 0.25 * jax.random.uniform(key_share, (BATCH, 1), jnp.float32, 0.4, 1.0) * (1.0 - 0.8 * position[:, None])
    common = jnp.sqrt(share) * base
    image = entry_scale * (common + jnp.sqrt(1.0 - share) * image_noise)
    text = entry_scale * (common + jnp.sqrt(1.0 - share) * text_noise)
    pair_index = index // 2
    chosen = pair_index % 61 == 7
    levels = jnp.array([5.0, 6.0, 7.0], jnp.float32)
    strength = levels[jax.random.randint(key_pick, (BATCH,), 0, 3)]
    strength_of = strength[pair_index][:, None]
    offset_gap = 0.1 / (entry_scale * entry_scale * E)
    previous = jnp.roll(text, 1, axis=0)
    first_one = (chosen & (index % 2 == 0))[:, None]
    second_one = (chosen & (index % 2 == 1))[:, None]
    new_text = jnp.where(second_one, (1.0 + offset_gap / strength_of) * previous, text)
    new_image = jnp.where(first_one, strength_of * text, jnp.where(second_one, (strength_of + offset_gap) * previous, image))
    return (jnp.clip(new_image, -4.0, 4.0), jnp.clip(new_text, -4.0, 4.0))


def draw_image(key, part):
    return paired(key)[0]


def draw_text(key, part):
    return paired(key)[1]


def setup_inputs(seed: int = 0) -> dict:
    keys = jax.random.split(jax.random.key(seed), 3)
    image = draw_image(jax.random.fold_in(keys[2], 71), 0)
    text = draw_text(jax.random.fold_in(keys[2], 71), 0)
    return {"image": image, "text": text}


logit_scale = 20.0


def reference(image, text):
    block_size = math.gcd(BATCH, 512)
    num_blocks = BATCH // block_size
    img_blocks = image.reshape(num_blocks, block_size, E)
    firsts = (jnp.arange(num_blocks) * block_size).astype(jnp.int32)
    col_ids = jnp.arange(BATCH).astype(jnp.int32)

    def logits_of(row_block):
        return logit_scale * jnp.dot(row_block, text.T, precision=lax.Precision.HIGHEST, preferred_element_type=jnp.float32)

    def col_step(state_pair, row_block):
        running_peak, running_total = state_pair
        scores = logits_of(row_block)
        latest = jnp.maximum(running_peak, jnp.max(scores, axis=0))
        running_total = running_total * jnp.exp(running_peak - latest) + jnp.sum(jnp.exp(scores - latest[None, :]), axis=0)
        return (latest, running_total), None

    start_state = (jnp.full((BATCH,), -jnp.inf, jnp.float32), jnp.zeros((BATCH,), jnp.float32))
    (col_peak, col_total), _ = lax.scan(col_step, start_state, img_blocks)
    col_lse = col_peak + jnp.log(col_total)

    def grad_step(state_pair, scan_items):
        text_acc, loss_acc = state_pair
        row_block, first_row = scan_items
        scores = logits_of(row_block)
        row_peak = jnp.max(scores, axis=1)
        row_lse = row_peak + jnp.log(jnp.sum(jnp.exp(scores - row_peak[:, None]), axis=1))
        row_ids = first_row + jnp.arange(block_size).astype(jnp.int32)
        is_diag = row_ids[:, None] == col_ids[None, :]
        weights = jnp.exp(scores - row_lse[:, None]) + jnp.exp(scores - col_lse[None, :]) - 2.0 * is_diag.astype(jnp.float32)
        image_part = 0.5 * logit_scale * jnp.dot(weights, text, precision=lax.Precision.HIGHEST, preferred_element_type=jnp.float32)
        text_acc = text_acc + 0.5 * logit_scale * jnp.dot(weights.T, row_block, precision=lax.Precision.HIGHEST, preferred_element_type=jnp.float32)
        diagonal_sum = jnp.sum(jnp.where(is_diag, scores, 0.0))
        loss_acc = loss_acc + jnp.sum(row_lse) - 2.0 * diagonal_sum
        return (text_acc, loss_acc), image_part

    init_pair = (jnp.zeros((BATCH, E), jnp.float32), jnp.zeros((), jnp.float32))
    (text_grad, loss_acc), image_parts = lax.scan(grad_step, init_pair, (img_blocks, firsts))
    loss = (loss_acc + jnp.sum(col_lse)) / (2.0 * BATCH)
    return (loss, image_parts.reshape(BATCH, E), text_grad)
```

```python
import functools
import jax
import jax.numpy as jnp
from jax import lax
from jax.experimental import pallas as pl
from jax.experimental.pallas import tpu as pltpu
from jax.sharding import PartitionSpec as P

logit_scale = 20.0
grad_scale = 0.5 * logit_scale
MESH = pl.DeviceIdType.MESH
XN = 4
CORES = 2
H = 16
G = 4 * H
f32 = jnp.float32
bf16 = jnp.bfloat16
NT = (((1,), (1,)), ((), ()))
NN = (((1,), (0,)), ((), ()))
TN = (((0,), (0,)), ((), ()))


def dot3(a_hi, a_lo, b_hi, b_lo, dims):
    def dot(a, b):
        return lax.dot_general(a, b, dims, preferred_element_type=f32)

    return dot(a_hi, b_hi) + (dot(a_hi, b_lo) + dot(a_lo, b_hi))


def split(value):
    high = value.astype(bf16)
    return high, (value - high.astype(f32)).astype(bf16)


def merge(parts):
    peak = functools.reduce(jnp.maximum, [p for p, _ in parts])
    total = functools.reduce(jnp.add, [t * jnp.exp(p - peak) for p, t in parts])
    return peak, total


class Comm:
    def __init__(self, send_sem, recv_sem):
        self.send_sem, self.recv_sem, self.copies = send_sem, recv_sem, []

    def send(self, src, dst, device):
        i = len(self.copies)
        copy = pltpu.make_async_remote_copy(
            src_ref=src,
            dst_ref=dst,
            send_sem=self.send_sem.at[i],
            recv_sem=self.recv_sem.at[i],
            device_id=device,
            device_id_type=MESH,
        )
        copy.start()
        self.copies.append(copy)
        return copy

    def drain(self):
        for copy in self.copies:
            copy.wait_send()


class Gather:
    def __init__(self, comm, buf, own, n, up, down, partner, other):
        self.comm, self.buf, self.n = comm, buf, n
        self.up, self.down, self.partner, self.other = up, down, partner, other
        self.ahead, self.behind = n // 2, n - 1 - n // 2
        buf[0, 0:H] = own[0:H]
        buf[0, 2 * H : 3 * H] = own[H : 2 * H]
        self.cross, self.ring_p, self.ring_q, self.core = {}, {}, {}, {}
        self.q_cross = self._copy(buf.at[0, 2 * H : 3 * H], buf.at[0, 3 * H : 4 * H], partner)
        self._forward(0, 0, self.ring_p, 0, 2 * H // 2)
        self._forward_back(0, self.ring_p, 0, H)
        self._cross(0)

    def _copy(self, src, dst, device):
        return self.comm.send(src, dst, device)

    def _forward(self, k, _, ring, lo, hi):
        if k < self.ahead:
            ring[k + 1] = self._copy(self.buf.at[k, lo:hi], self.buf.at[k + 1, lo:hi], self.down)

    def _forward_back(self, k, ring, lo, hi):
        if k < self.behind:
            src, dst = (self.n - k) % self.n, self.n - k - 1
            ring[dst] = self._copy(self.buf.at[src, lo:hi], self.buf.at[dst, lo:hi], self.up)

    def _cross(self, k):
        self.cross[k] = self._copy(self.buf.at[k, 0:H], self.buf.at[k, H : 2 * H], self.partner)

    def start_q(self):
        self.q_cross.wait_recv()
        self._forward(0, 0, self.ring_q, 2 * H, G)
        self._forward_back(0, self.ring_q, 2 * H, G)

    def positions(self, s):
        if s == 0:
            return [0]
        return [s] + ([self.n - s] if s <= self.behind else [])

    def step_p(self, s):
        for k in self.positions(s):
            self.ring_p[k].wait_recv()
            if k == s:
                self._forward(k, 0, self.ring_p, 0, H)
            else:
                self._forward_back(s, self.ring_p, 0, H)
            self._cross(k)

    def step_q(self, s):
        for k in self.positions(s):
            self.ring_q[k].wait_recv()
            if k == s:
                self._forward(k, 0, self.ring_q, 2 * H, G)
            else:
                self._forward_back(s, self.ring_q, 2 * H, G)

    def finish(self, s):
        for k in self.positions(s):
            self.cross[k].wait_recv()
            if self.other is not None:
                to = (self.n - k) % self.n
                self.core[to] = self._copy(self.buf.at[k, 0:G], self.buf.at[to, G : 2 * G], self.other)


class Scatter:
    def __init__(self, comm, acc, cross_buf, p_up, p_down, q_up, q_down, q_cross, n, up, down, partner):
        self.comm, self.acc, self.cross_buf, self.n = comm, acc, cross_buf, n
        self.bufs = {"p": (p_up, p_down), "q": (q_up, q_down)}
        self.q_cross_buf = q_cross
        self.up, self.down, self.partner = up, down, partner
        self.ahead, self.behind = n // 2, n - 1 - n // 2
        self.cross, self.rings = {}, {}

    def rows(self, half):
        return slice(0, H) if half == "p" else slice(2 * H, G)

    def send_cross(self, k):
        self.cross[k] = self.comm.send(self.acc.at[k, H : 2 * H], self.cross_buf.at[k], self.partner)

    def add_cross(self, k):
        self.cross[k].wait_recv()
        self.acc[k, 0:H] += self.cross_buf[k]

    def launch(self, half, k):
        rows = self.rows(half)
        if k <= self.ahead:
            buf, step, device, key = self.bufs[half][0], self.ahead - k, self.up, (half, k - 1)
        else:
            back = self.n - k
            buf, step, device = self.bufs[half][1], self.behind - back, self.down
            key = (half, (k + 1) % self.n, "back")
        self.rings[key] = (self.comm.send(self.acc.at[k, rows], buf.at[step], device), buf, step)

    def take(self, half, k, back=False):
        key = (half, k, "back") if back else (half, k)
        copy, buf, step = self.rings[key]
        copy.wait_recv()
        self.acc[k, self.rows(half)] += buf[step]

    def step(self, half, s):
        k = self.ahead - s
        if k >= 0:
            self.take(half, k)
            if k > 0:
                self.launch(half, k)
        back = self.behind - s
        if back >= 0 and self.behind > 0:
            k = (self.n - back) % self.n
            self.take(half, k, True)
            if k:
                self.launch(half, k)

    def finish_q(self):
        self.last = self.comm.send(self.acc.at[0, 3 * H : 4 * H], self.q_cross_buf, self.partner)

    def result(self, out):
        out[0:H] = self.acc[0, 0:H] * grad_scale
        self.last.wait_recv()
        out[H : 2 * H] = (self.acc[0, 2 * H : 3 * H] + self.q_cross_buf[...]) * grad_scale


def kernel(nz, ny, image, text, loss, image_grad, text_grad,
           T, I, Th, Tl, Ih, Il, L, Er, Wh, Wl, TP, CR, IP,
           tx, tpu_, tpd, tqu, tqd, tqx, ix, ipu, ipd, iqu, iqd, iqx,
           St, Si, R1t, R1i, R2t, R2i, Ft, Fi, L1, L2, L3, send_sem, recv_sem):
    row, y = lax.axis_index("row"), lax.axis_index("col")
    x, z, c = row // (CORES * nz), (row // CORES) % nz, row % CORES
    turn = 1 - 2 * c
    xt = x + 1 - 2 * (x % 2)
    xi = XN - 1 - x

    def at(x_=x, y_=y, z_=z, c_=c):
        return (x_ * (CORES * nz) + z_ * CORES + c_, y_)

    def ring_z(k):
        return at(z_=(z + turn * k + nz) % nz)

    def ring_y(k):
        return at(y_=(y + turn * k + ny) % ny)

    def plane(i):
        j = (x * CORES + c + i) % (XN * CORES)
        return at(x_=j // CORES, c_=j % CORES)

    other = at(c_=1 - c)
    cols, rws = nz * 2 * G, ny * G
    comm = Comm(send_sem, recv_sem)

    barrier = pltpu.get_barrier_semaphore()
    peers = [ring_z(k) for k in range(1, nz)] + [ring_y(k) for k in range(1, ny)]
    peers += [plane(i) for i in range(1, XN * CORES)]
    for peer in peers:
        pl.semaphore_signal(barrier, inc=1, device_id=peer, device_id_type=MESH)
    pl.semaphore_wait(barrier, len(peers))

    gt = Gather(comm, T, text, nz, ring_z(1), ring_z(nz - 1), at(x_=xt), other)
    gi = Gather(comm, I, image, ny, ring_y(1), ring_y(ny - 1), at(x_=xi), None)
    gt.start_q()
    gi.start_q()
    steps = max(nz, ny) // 2 + 1
    for s in range(steps):
        for g in (gt, gi):
            if 1 <= s <= g.ahead:
                g.step_p(s)
        for g in (gt, gi):
            if 1 <= s <= g.ahead:
                g.step_q(s)
        for g in (gt, gi):
            if s <= g.ahead:
                g.finish(s)
    for k in range(ny):
        Ih[k * G : (k + 1) * G], Il[k * G : (k + 1) * G] = split(I[k])
    for k in range(nz):
        gt.core[k].wait_recv()
        first = k * 2 * G
        Th[first : first + 2 * G], Tl[first : first + 2 * G] = split(T[k])

    block = min(256, cols)
    blocks = cols // block
    for b in range(blocks):
        span = slice(b * block, (b + 1) * block)
        L[:, span] = logit_scale * dot3(Ih[...], Il[...], Th[span], Tl[span], NT)

    def iota(shape, dim):
        return lax.broadcasted_iota(jnp.int32, shape, dim)

    lane = iota((1, cols), 1)
    at_z = (z + turn * (lane >> 7) + nz) & (nz - 1)
    at_x = jnp.where((lane >> 4) & 1 == 0, x, xt)
    at_c = jnp.where((lane >> 6) & 1 == 0, c, 1 - c)
    col_ids = (
        y * (XN * nz * CORES * 2 * H)
        + ((at_x * nz + at_z) * CORES + at_c) * (2 * H)
        + ((lane >> 5) & 1) * H
        + (lane & 15)
    )

    def row_ids(k):
        r = iota((G, 1), 0)
        of_x = jnp.where((r >> 4) & 1 == 0, x, xi)
        of_y = (y + turn * k + ny) & (ny - 1)
        return ((of_x * nz + z) * CORES + c) * (ny * 2 * H) + of_y * (2 * H) + ((r >> 5) & 1) * H + (r & 15)

    own_lane = iota((G, 128), 0) == iota((G, 128), 1)

    def to_lanes(column):
        return jnp.sum(jnp.where(own_lane, column, 0.0), axis=0, keepdims=True)

    def to_column(lanes):
        return jnp.sum(jnp.where(own_lane, lanes, 0.0), axis=1, keepdims=True)

    def group8(v, op):
        return op(v.reshape(v.shape[0] // 8, 8, v.shape[1]), axis=0)

    def row_pass(k, carry):
        peak, diag = carry
        here = pl.ds(pl.multiple_of(k * G, G), G)
        tile = L[here]
        row_peak = jnp.max(tile, axis=1, keepdims=True)
        terms = jnp.exp(tile - row_peak)
        Er[here] = terms
        Si[0, pl.ds(k, 1)] = to_lanes(row_peak)
        Si[1, pl.ds(k, 1)] = to_lanes(jnp.sum(terms, axis=1, keepdims=True))
        diag = diag + group8(jnp.where(row_ids(k) == col_ids, tile, 0.0), jnp.sum)
        return jnp.maximum(peak, group8(tile, jnp.max)), diag

    start = (jnp.full((8, cols), -jnp.inf, f32), jnp.zeros((8, cols), f32))
    peak8, diag8 = lax.fori_loop(0, ny, row_pass, start)
    col_peak = jnp.max(peak8, axis=0, keepdims=True)
    lanes_n = cols // 128
    diag_sum = functools.reduce(jnp.add, [diag8[:, i * 128 : (i + 1) * 128] for i in range(lanes_n)])

    def col_pass(k, total):
        here = pl.ds(pl.multiple_of(k * G, G), G)
        terms = jnp.exp(L[here] - col_peak)
        L[here] = terms
        return total + group8(terms, jnp.sum)

    col_total = jnp.sum(lax.fori_loop(0, ny, col_pass, jnp.zeros((8, cols), f32)), axis=0, keepdims=True)

    def fold(v):
        return jnp.concatenate([v[:, k * 128 : (k + 1) * 128] for k in range(nz)], axis=0)

    St[0], St[1] = fold(col_peak), fold(col_total)

    at_xt, at_xi = at(x_=xt), at(x_=xi)
    near = [
        comm.send(St, R1t.at[0], at_xt),
        comm.send(Si, R1i, at_xi),
        comm.send(St, R1t.at[1], other),
        comm.send(St, R1t.at[2], at(x_=xt, c_=1 - c)),
    ]
    lane_n = iota((nz, 128), 1)

    def swap_x(v):
        low = (iota(v.shape, 1) >> 4) & 1 == 0
        return jnp.where(low, pltpu.roll(v, 128 - H, 1), pltpu.roll(v, H, 1))

    def swap_core(v):
        v = pltpu.roll(v, G, 1)
        return jnp.concatenate([v[(nz - k) % nz : (nz - k) % nz + 1] for k in range(nz)], axis=0)

    def shift(v, k, n):
        return jnp.concatenate([v[n - k :], v[: n - k]], axis=0)

    peak_t, total_t = St[0], St[1]
    valid_i = iota((ny, 128), 1) < G
    peak_i, total_i = Si[0], jnp.where(valid_i, Si[1], 1.0)
    for copy in near:
        copy.wait_recv()
    pt, tt = merge([
        (peak_t, total_t),
        (swap_x(R1t[0, 0]), swap_x(R1t[0, 1])),
        (swap_core(R1t[1, 0]), swap_core(R1t[1, 1])),
        (swap_x(swap_core(R1t[2, 0])), swap_x(swap_core(R1t[2, 1]))),
    ])
    pi, ti = merge([(peak_i, total_i), (swap_x(R1i[0]), jnp.where(valid_i, swap_x(R1i[1]), 1.0))])
    R2t[0, 0], R2t[0, 1] = pt, tt
    R2i[0, 0], R2i[0, 1] = pi, ti
    far = [comm.send(R2t.at[0], R2t.at[nz - k], ring_z(k)) for k in range(1, nz)]
    far += [comm.send(R2i.at[0], R2i.at[ny - k], ring_y(k)) for k in range(1, ny)]
    for copy in far:
        copy.wait_recv()
    pt, tt = merge([(pt, tt)] + [(shift(R2t[k, 0], k, nz), shift(R2t[k, 1], k, nz)) for k in range(1, nz)])
    pi, ti = merge([(pi, ti)] + [(shift(R2i[k, 0], k, ny), shift(R2i[k, 1], k, ny)) for k in range(1, ny)])
    Ft[...] = jnp.exp(peak_t - pt) / tt
    Fi[...] = jnp.exp(peak_i - pi) / ti

    def own(v):
        i = iota(v.shape, 1)
        mine = (iota(v.shape, 0) == 0) & (i < G) & ((i >> 4) & 1 == 0)
        return jnp.sum(jnp.where(mine, v, 0.0), axis=0, keepdims=True)

    first = iota((8, 128), 0) == 0
    part = own(pt + jnp.log(tt)) + own(pi + jnp.log(ti))
    L1[x * CORES + c] = jnp.where(first, part, 0.0) - 2.0 * diag_sum
    l1 = [comm.send(L1.at[x * CORES + c], L1.at[x * CORES + c], plane(i)) for i in range(1, XN * CORES)]

    col_factor = jnp.concatenate([Ft[k : k + 1] for k in range(nz)], axis=1)

    def weigh(k, _):
        here = pl.ds(pl.multiple_of(k * G, G), G)
        value = Er[here] * to_column(Fi[pl.ds(k, 1)]) + L[here] * col_factor
        value = value - jnp.where(row_ids(k) == col_ids, 2.0, 0.0)
        Wh[here], Wl[here] = split(value)
        return 0

    lax.fori_loop(0, ny, weigh, 0)

    st = Scatter(comm, TP, tx, tpu_, tpd, tqu, tqd, tqx, nz, ring_z(1), ring_z(nz - 1), at(x_=xt))
    si = Scatter(comm, IP, ix, ipu, ipd, iqu, iqd, iqx, ny, ring_y(1), ring_y(ny - 1), at(x_=xi))
    core = {}
    per = block // 128
    order = sorted(range(blocks), key=lambda b: abs(b * per - nz // 2))
    for b in order:
        span = slice(b * block, (b + 1) * block)
        part = dot3(Wh[:, span], Wl[:, span], Ih[...], Il[...], TN)
        for k in range(b * per, (b + 1) * per):
            TP[k] = part[(k - b * per) * 128 : (k - b * per + 1) * 128]
            to = (nz - k) % nz
            core[to] = comm.send(TP.at[k, G : 2 * G], CR.at[to], other)
    half = rws // 2
    for b in (1, 0):
        part = dot3(Wh[b * half : (b + 1) * half], Wl[b * half : (b + 1) * half], Th[...], Tl[...], NN)
        for k in range(ny // 2):
            IP[b * (ny // 2) + k] = part[k * G : (k + 1) * G]
        for k in range(b * (ny // 2), (b + 1) * (ny // 2)):
            si.send_cross(k)
        if b == 1:
            si.launch("q", ny // 2)
            if ny // 2 + 1 < ny:
                si.launch("q", ny // 2 + 1)
    far_first = lambda n: sorted(range(n), key=lambda k: -min(k, n - k))
    for k in far_first(nz):
        core[k].wait_recv()
        TP[k, 0:G] += CR[k]
        st.send_cross(k)
        if k == nz // 2 or k == nz // 2 + 1:
            st.launch("q", k)
    for copy in l1:
        copy.wait_recv()
    L2[y] = functools.reduce(jnp.add, [L1[i] for i in range(XN * CORES)])
    l2 = [comm.send(L2.at[y], L2.at[y], ring_y(k)) for k in range(1, ny)]
    for n, sc in ((ny, si), (nz, st)):
        for k in (n // 2, n // 2 + 1):
            if k < n:
                sc.add_cross(k)
                sc.launch("p", k)
    for n, sc in ((ny, si), (nz, st)):
        for k in far_first(n):
            if k != n // 2 and k != n // 2 + 1:
                sc.add_cross(k)
    for copy in l2:
        copy.wait_recv()
    L3[z] = functools.reduce(jnp.add, [L2[i] for i in range(ny)])
    l3 = [comm.send(L3.at[z], L3.at[z], ring_z(k)) for k in range(1, nz)]
    for s in range(1, max(ny, nz) // 2 + 1):
        for n, sc in ((ny, si), (nz, st)):
            if s <= n // 2:
                sc.step("q", s)
                sc.step("p", s)
    si.finish_q()
    st.finish_q()
    for copy in l3:
        copy.wait_recv()
    samples = XN * nz * CORES * ny * 2 * H
    loss[0, 0] = jnp.sum(functools.reduce(jnp.add, [L3[i] for i in range(nz)])) / (2.0 * samples)
    si.result(image_grad)
    st.result(text_grad)
    comm.drain()


def local(image, text):
    nz = lax.axis_size("row") // (XN * CORES)
    ny = lax.axis_size("col")
    E = image.shape[1]
    cols, rws = nz * 2 * G, ny * G
    vmem = lambda *shape, dtype=f32: pltpu.VMEM(shape, dtype)

    def ring(n):
        ahead, behind = n // 2, max(n - 1 - n // 2, 1)
        return [
            vmem(n, H, E),
            vmem(ahead, H, E),
            vmem(behind, H, E),
            vmem(ahead, 2 * H, E),
            vmem(behind, 2 * H, E),
            vmem(H, E),
        ]

    scratch = [
        vmem(nz, 2 * G, E),
        vmem(ny, G, E),
        vmem(cols, E, dtype=bf16),
        vmem(cols, E, dtype=bf16),
        vmem(rws, E, dtype=bf16),
        vmem(rws, E, dtype=bf16),
        vmem(rws, cols),
        vmem(rws, cols),
        vmem(rws, cols, dtype=bf16),
        vmem(rws, cols, dtype=bf16),
        vmem(nz, 2 * G, E),
        vmem(nz, G, E),
        vmem(ny, G, E),
        *ring(nz),
        *ring(ny),
        vmem(2, nz, 128),
        vmem(2, ny, 128),
        vmem(3, 2, nz, 128),
        vmem(2, ny, 128),
        vmem(nz, 2, nz, 128),
        vmem(ny, 2, ny, 128),
        vmem(nz, 128),
        vmem(ny, 128),
        vmem(XN * CORES, 8, 128),
        vmem(ny, 8, 128),
        vmem(nz, 8, 128),
        pltpu.SemaphoreType.DMA((160,)),
        pltpu.SemaphoreType.DMA((160,)),
    ]
    block = pl.BlockSpec(memory_space=pltpu.VMEM)
    loss, image_grad, text_grad = pl.pallas_call(
        functools.partial(kernel, nz, ny),
        out_shape=(
            jax.ShapeDtypeStruct((1, 1), f32),
            jax.ShapeDtypeStruct(image.shape, f32),
            jax.ShapeDtypeStruct(text.shape, f32),
        ),
        in_specs=[block, block],
        out_specs=(pl.BlockSpec(memory_space=pltpu.SMEM), block, block),
        scratch_shapes=scratch,
        compiler_params=pltpu.CompilerParams(
            collective_id=0, has_side_effects=True, vmem_limit_bytes=48 * 1024 * 1024
        ),
        name="contrastive",
    )(image, text)
    return loss.reshape(()), image_grad, text_grad


def solution(mesh):
    in_specs = (P(("row", "col"), None), P(("col", "row"), None))
    out_specs = (P(), P(("row", "col"), None), P(("col", "row"), None))
    return jax.shard_map(local, mesh=mesh, in_specs=in_specs, out_specs=out_specs, check_vma=False)
```

```python
import functools
import jax
import jax.numpy as jnp
from jax import lax
from jax.experimental import pallas as pl
from jax.experimental.pallas import tpu as pltpu
from jax.sharding import PartitionSpec as P

logit_scale = 20.0
grad_scale = 0.5 * logit_scale
MESH = pl.DeviceIdType.MESH
XN = 4
CORES = 2
H = 16
TREES = ((0, 0, 1, 2, 3), None, (0, 0, 1, 2, 3), (0, 0, 1, 2, 3))
MESSAGES = 76
SMALL = 39
G = 4 * H
f32 = jnp.float32
bf16 = jnp.bfloat16
NT = (((1,), (1,)), ((), ()))
NN = (((1,), (0,)), ((), ()))
TN = (((0,), (0,)), ((), ()))


def dot3(a_hi, a_lo, b_hi, b_lo, dims):
    def dot(a, b):
        return lax.dot_general(a, b, dims, preferred_element_type=f32)

    return dot(a_hi, b_hi) + (dot(a_hi, b_lo) + dot(a_lo, b_hi))


def split(value):
    high = value.astype(bf16)
    return high, (value - high.astype(f32)).astype(bf16)


def merge(parts):
    peak = functools.reduce(jnp.maximum, [p for p, _ in parts])
    total = functools.reduce(jnp.add, [t * jnp.exp(p - peak) for p, t in parts])
    return peak, total


class Comm:
    def __init__(self, send_sem, recv_sem):
        self.send_sem, self.recv_sem, self.next = send_sem, recv_sem, 0

    def send(self, src, dst, device, group):
        copy = pltpu.make_async_remote_copy(
            src_ref=src,
            dst_ref=dst,
            send_sem=self.send_sem.at[group],
            recv_sem=self.recv_sem.at[self.next],
            device_id=device,
            device_id_type=MESH,
        )
        copy.start()
        self.next += 1
        return copy

    def sent(self, group, like, device):
        pltpu.make_async_remote_copy(
            src_ref=like,
            dst_ref=like,
            send_sem=self.send_sem.at[group],
            recv_sem=self.recv_sem.at[0],
            device_id=device,
            device_id_type=MESH,
        ).wait_send()


class Trees:
    def __init__(self, n):
        self.n, self.ahead, self.behind = n, n // 2, n - 1 - n // 2

    def parent(self, lo, d):
        return TREES[lo // H][d]

    def side(self, k):
        return (k, 1, self.ahead) if k <= self.ahead else (self.n - k, -1, self.behind)

    def sides(self, k):
        return [(0, 1, self.ahead), (0, -1, self.behind)] if k == 0 else [self.side(k)]

    def children(self, lo, d, most):
        return [c for c in range(most, d, -1) if self.parent(lo, c) == d]

    def slot(self, d, way):
        return (way * d) % self.n


class Gather(Trees):
    def __init__(self, comm, buf, n, ring, partner, other, group):
        super().__init__(n)
        self.comm, self.buf, self.at, self.partner, self.other, self.group = comm, buf, ring, partner, other, group
        self.cross, self.ring, self.core = {}, {}, {}

    def start(self):
        self.q_cross = self.comm.send(
            self.buf.at[0, 2 * H : 3 * H], self.buf.at[0, 3 * H : G], self.partner, self.group
        )
        self.forward(0, 0)
        self.send_cross(0)
        self.forward(0, 2 * H)

    def start_cross(self):
        self.q_cross.wait_recv()
        self.forward(0, 3 * H)

    def forward(self, k, lo):
        for d, way, most in self.sides(k):
            for c in self.children(lo, d, most):
                to = self.slot(c, way)
                self.ring[to, lo] = self.comm.send(
                    self.buf.at[k, lo : lo + H],
                    self.buf.at[to, lo : lo + H],
                    self.at((-way * (c - d)) % self.n),
                    self.group,
                )

    def send_cross(self, k):
        self.cross[k] = self.comm.send(
            self.buf.at[k, 0:H], self.buf.at[k, H : 2 * H], self.partner, self.group
        )

    def positions(self, s):
        if s > self.ahead:
            return []
        return sorted({s % self.n, (self.n - s) % self.n} if s <= self.behind else {s})

    def step(self, s, lo):
        for k in self.positions(s):
            self.ring[k, lo].wait_recv()
            self.forward(k, lo)
            if lo == 0:
                self.send_cross(k)

    def pass_core(self, k, lo):
        if self.other is not None:
            to = (self.n - k) % self.n
            self.core[to, lo] = self.comm.send(
                self.buf.at[k, lo : lo + 2 * H], self.buf.at[to, G + lo : G + lo + 2 * H], self.other, 1
            )

    def finish_q(self, s):
        for k in self.positions(s):
            self.pass_core(k, 2 * H)

    def finish_p(self, s):
        for k in self.positions(s):
            self.cross[k].wait_recv()
            self.pass_core(k, 0)


class Scatter(Trees):
    def __init__(self, comm, acc, cross_buf, up_buf, down_buf, q_cross, n, ring, partner, group):
        super().__init__(n)
        self.comm, self.acc, self.cross_buf = comm, acc, cross_buf
        self.bufs, self.q_cross_buf = {1: up_buf, -1: down_buf}, q_cross
        self.at, self.partner, self.group = ring, partner, group
        self.cross, self.rings = {}, {}
        self.far = sorted(range(n), key=lambda k: -min(k, n - k))

    def send_cross(self, k):
        self.cross[k] = self.comm.send(
            self.acc.at[k, H : 2 * H], self.cross_buf.at[k], self.partner, self.group
        )

    def leaf(self, k, lo):
        return not any(self.children(lo, d, most) for d, _, most in self.sides(k))

    def launch(self, k, lo):
        d, way, _ = self.side(k)
        dst = self.bufs[way].at[d - 1, lo : lo + H]
        to = self.at((way * (d - self.parent(lo, d))) % self.n)
        copy = self.comm.send(self.acc.at[k, lo : lo + H], dst, to, self.group)
        self.rings[way, d, lo] = (copy, dst)

    def begin(self, ks):
        for k in ks:
            self.send_cross(k)
        for k in ks:
            for lo in (3 * H, 2 * H):
                if self.leaf(k, lo):
                    self.launch(k, lo)

    def step(self, k, lo):
        if lo == 0:
            self.cross[k].wait_recv()
            self.acc[k, 0:H] += self.cross_buf[k]
            if self.leaf(k, lo):
                self.launch(k, lo)
        if self.leaf(k, lo):
            return
        for d, way, most in self.sides(k):
            for c in self.children(lo, d, most):
                copy, dst = self.rings[way, c, lo]
                copy.wait_recv()
                self.acc[k, lo : lo + H] += dst[...]
        if k:
            self.launch(k, lo)
        elif lo == 3 * H:
            self.last = self.comm.send(self.acc.at[0, lo:G], self.q_cross_buf, self.partner, self.group)

    def result(self, out):
        out[0:H] = self.acc[0, 0:H]
        self.last.wait_recv()
        out[H : 2 * H] = self.acc[0, 2 * H : 3 * H] + self.q_cross_buf[...]


def kernel(nz, ny, image, text, loss, image_grad, text_grad,
           T, I, Th, Tl, Ih, Il, L, Er, Wh, Wl, TP, CR, IP,
           tx, tu, td, tq, ix, iu, id_, iq,
           St, Si, R1t, R1i, R2t, R2i, Ft, Fi, L1, L2, L3, send_sem, recv_sem, own_sem):
    row, y = lax.axis_index("row"), lax.axis_index("col")
    x, z, c = row // (CORES * nz), (row // CORES) % nz, row % CORES
    turn = 1 - 2 * c
    xt = x + 1 - 2 * (x % 2)
    xi = XN - 1 - x

    def at(x_=x, y_=y, z_=z, c_=c):
        return (x_ * (CORES * nz) + z_ * CORES + c_, y_)

    def ring_z(k):
        return at(z_=(z + turn * k + nz) % nz)

    def ring_y(k):
        return at(y_=(y + turn * k + ny) % ny)

    def plane(i):
        j = (x * CORES + c + i) % (XN * CORES)
        return at(x_=j // CORES, c_=j % CORES)

    other = at(c_=1 - c)
    cols, rws = nz * 2 * G, ny * G
    comm = Comm(send_sem, recv_sem)

    own_copies = [
        pltpu.make_async_copy(src.at[h * H : (h + 1) * H], dst.at[0, 2 * h * H : (2 * h + 1) * H], own_sem.at[i, h])
        for i, (src, dst) in enumerate(((text, T), (image, I)))
        for h in (1, 0)
    ]
    for copy in own_copies:
        copy.start()
    barrier = pltpu.get_barrier_semaphore()
    peers = [ring_z(k) for k in range(1, nz)] + [ring_y(k) for k in range(1, ny)]
    peers += [plane(i) for i in range(1, XN * CORES)]
    for peer in peers:
        pl.semaphore_signal(barrier, inc=1, device_id=peer, device_id_type=MESH)
    for copy in own_copies:
        copy.wait()
    pl.semaphore_wait(barrier, len(peers))

    gt = Gather(comm, T, nz, ring_z, at(x_=xt), other, 0)
    gi = Gather(comm, I, ny, ring_y, at(x_=xi), None, 2)
    both = (gt, gi)
    for g in both:
        g.start()
    for g in both:
        g.start_cross()
    for s in range(max(nz, ny) // 2 + 1):
        for lo in (0, 2 * H, 3 * H):
            for g in both:
                if s:
                    g.step(s, lo)
        for g in both:
            g.finish_q(s)
            if s:
                g.finish_p(s - 1)

    block = min(256, cols)
    blocks = cols // block
    per = block // 128
    half = ny // 2
    distance = lambda k, n: min(k, n - k)
    near_first = sorted(range(blocks), key=lambda b: max(distance(k, nz) for k in range(b * per, (b + 1) * per)))

    def take_image(h):
        for k in range(h * half, (h + 1) * half):
            Ih[k * G : (k + 1) * G], Il[k * G : (k + 1) * G] = split(I[k])

    def take_text(b):
        for k in range(b * per, (b + 1) * per):
            gt.core[k, 0].wait_recv()
            gt.core[k, 2 * H].wait_recv()
            first = k * 2 * G
            Th[first : first + 2 * G], Tl[first : first + 2 * G] = split(T[k])

    def logits(rows, b):
        span = slice(b * block, (b + 1) * block)
        L[rows, span] = logit_scale * dot3(Ih[rows], Il[rows], Th[span], Tl[span], NT)

    low, high = slice(0, half * G), slice(half * G, rws)
    take_image(0)
    for b in near_first[:-1]:
        take_text(b)
        logits(low, b)
    for g in both:
        g.finish_p(g.ahead)
    take_image(1)
    for b in near_first[:-1]:
        logits(high, b)
    take_text(near_first[-1])
    logits(slice(0, rws), near_first[-1])

    def all_sent():
        comm.sent(0, T.at[0 : nz // 2, 0 : 2 * G - G // nz], other)
        comm.sent(1, T.at[0 : nz // 2], other)
        comm.sent(2, T.at[0 : ny // 2, 0 : 2 * G - G // ny], other)

    all_sent()
    comm.next = MESSAGES

    def iota(shape, dim):
        return lax.broadcasted_iota(jnp.int32, shape, dim)

    lane = iota((1, cols), 1)
    at_z = (z + turn * (lane >> 7) + nz) & (nz - 1)
    at_x = jnp.where((lane >> 4) & 1 == 0, x, xt)
    at_c = jnp.where((lane >> 6) & 1 == 0, c, 1 - c)
    col_ids = (
        y * (XN * nz * CORES * 2 * H)
        + ((at_x * nz + at_z) * CORES + at_c) * (2 * H)
        + ((lane >> 5) & 1) * H
        + (lane & 15)
    )

    def row_ids(k):
        r = iota((G, 1), 0)
        of_x = jnp.where((r >> 4) & 1 == 0, x, xi)
        of_y = (y + turn * k + ny) & (ny - 1)
        return ((of_x * nz + z) * CORES + c) * (ny * 2 * H) + of_y * (2 * H) + ((r >> 5) & 1) * H + (r & 15)

    own_lane = iota((G, 128), 0) == iota((G, 128), 1)

    def to_lanes(column):
        return jnp.sum(jnp.where(own_lane, column, 0.0), axis=0, keepdims=True)

    def to_column(lanes):
        return jnp.sum(jnp.where(own_lane, lanes, 0.0), axis=1, keepdims=True)

    def group8(v, op):
        return op(v.reshape(v.shape[0] // 8, 8, v.shape[1]), axis=0)

    def row_pass(k, carry):
        peak, diag = carry
        here = pl.ds(pl.multiple_of(k * G, G), G)
        tile = L[here]
        row_peak = jnp.max(tile, axis=1, keepdims=True)
        terms = jnp.exp(tile - row_peak)
        Er[here] = terms
        Si[0, pl.ds(k, 1)] = to_lanes(row_peak)
        Si[1, pl.ds(k, 1)] = to_lanes(jnp.sum(terms, axis=1, keepdims=True))
        diag = diag + group8(jnp.where(row_ids(k) == col_ids, tile, 0.0), jnp.sum)
        return jnp.maximum(peak, group8(tile, jnp.max)), diag

    start = (jnp.full((8, cols), -jnp.inf, f32), jnp.zeros((8, cols), f32))
    peak8, diag8 = lax.fori_loop(0, ny, row_pass, start)
    col_peak = jnp.max(peak8, axis=0, keepdims=True)
    lanes_n = cols // 128
    diag_sum = functools.reduce(jnp.add, [diag8[:, i * 128 : (i + 1) * 128] for i in range(lanes_n)])

    def col_pass(k, total):
        here = pl.ds(pl.multiple_of(k * G, G), G)
        terms = jnp.exp(L[here] - col_peak)
        L[here] = terms
        return total + group8(terms, jnp.sum)

    col_total = jnp.sum(lax.fori_loop(0, ny, col_pass, jnp.zeros((8, cols), f32)), axis=0, keepdims=True)

    def fold(v):
        return jnp.concatenate([v[:, k * 128 : (k + 1) * 128] for k in range(nz)], axis=0)

    St[0], St[1] = fold(col_peak), fold(col_total)

    at_xt, at_xi = at(x_=xt), at(x_=xi)
    near = [
        comm.send(St, R1t.at[0], at_xt, 3),
        comm.send(Si, R1i, at_xi, 7),
        comm.send(St, R1t.at[1], other, 3),
        comm.send(St, R1t.at[2], at(x_=xt, c_=1 - c), 3),
    ]
    lane_n = iota((nz, 128), 1)

    def swap_x(v):
        low = (iota(v.shape, 1) >> 4) & 1 == 0
        return jnp.where(low, pltpu.roll(v, 128 - H, 1), pltpu.roll(v, H, 1))

    def swap_core(v):
        v = pltpu.roll(v, G, 1)
        return jnp.concatenate([v[(nz - k) % nz : (nz - k) % nz + 1] for k in range(nz)], axis=0)

    def shift(v, k, n):
        return jnp.concatenate([v[n - k :], v[: n - k]], axis=0)

    peak_t, total_t = St[0], St[1]
    valid_i = iota((ny, 128), 1) < G
    peak_i, total_i = Si[0], jnp.where(valid_i, Si[1], 1.0)
    for copy in near:
        copy.wait_recv()
    pt, tt = merge([
        (peak_t, total_t),
        (swap_x(R1t[0, 0]), swap_x(R1t[0, 1])),
        (swap_core(R1t[1, 0]), swap_core(R1t[1, 1])),
        (swap_x(swap_core(R1t[2, 0])), swap_x(swap_core(R1t[2, 1]))),
    ])
    pi, ti = merge([(peak_i, total_i), (swap_x(R1i[0]), jnp.where(valid_i, swap_x(R1i[1]), 1.0))])
    R2t[0, 0], R2t[0, 1] = pt, tt
    R2i[0, 0], R2i[0, 1] = pi, ti
    far = [comm.send(R2t.at[0], R2t.at[nz - k], ring_z(k), 8) for k in range(1, nz)]
    far += [comm.send(R2i.at[0], R2i.at[ny - k], ring_y(k), 9) for k in range(1, ny)]
    for copy in far:
        copy.wait_recv()
    pt, tt = merge([(pt, tt)] + [(shift(R2t[k, 0], k, nz), shift(R2t[k, 1], k, nz)) for k in range(1, nz)])
    pi, ti = merge([(pi, ti)] + [(shift(R2i[k, 0], k, ny), shift(R2i[k, 1], k, ny)) for k in range(1, ny)])
    Ft[...] = jnp.exp(peak_t - pt) / tt
    Fi[...] = jnp.exp(peak_i - pi) / ti

    def own(v):
        i = iota(v.shape, 1)
        mine = (iota(v.shape, 0) == 0) & (i < G) & ((i >> 4) & 1 == 0)
        return jnp.sum(jnp.where(mine, v, 0.0), axis=0, keepdims=True)

    first = iota((8, 128), 0) == 0
    part = own(pt + jnp.log(tt)) + own(pi + jnp.log(ti))
    L1[x * CORES + c] = jnp.where(first, part, 0.0) - 2.0 * diag_sum
    l1 = [comm.send(L1.at[x * CORES + c], L1.at[x * CORES + c], plane(i), 4) for i in range(1, XN * CORES)]

    col_factor = jnp.concatenate([Ft[k : k + 1] for k in range(nz)], axis=1)

    def weigh(k, _):
        here = pl.ds(pl.multiple_of(k * G, G), G)
        value = Er[here] * to_column(Fi[pl.ds(k, 1)]) + L[here] * col_factor
        value = value - jnp.where(row_ids(k) == col_ids, 2.0, 0.0)
        Wh[here], Wl[here] = split(value)
        return 0

    lax.fori_loop(0, ny, weigh, 0)

    small, comm.next = comm.next, 0
    st = Scatter(comm, TP, tx, tu, td, tq, nz, ring_z, at(x_=xt), 0)
    si = Scatter(comm, IP, ix, iu, id_, iq, ny, ring_y, at(x_=xi), 2)
    core, done, added = {}, [], []

    def gradients(b):
        span = slice(b * block, (b + 1) * block)
        part = dot3(Wh[:, span], Wl[:, span], Ih[...], Il[...], TN)
        here = list(range(b * per, (b + 1) * per))
        for i, k in enumerate(here):
            TP[k] = part[i * 128 : (i + 1) * 128]
            to = (nz - k) % nz
            core[to] = comm.send(TP.at[k, G : 2 * G], CR.at[to], other, 1)
        rows = slice(here[0] * G, (here[-1] + 1) * G)
        part = dot3(Wh[rows], Wl[rows], Th[...], Tl[...], NN)
        for i, k in enumerate(here):
            IP[k] = part[i * G : (i + 1) * G]
        si.begin([k for k in si.far if k in here])
        done.extend(here)
        ready = [k for k in st.far if k in done and (nz - k) % nz in done and k not in added]
        for k in ready:
            core[k].wait_recv()
            TP[k, 0:G] += CR[k]
        added.extend(ready)
        st.begin(ready)

    steps = [(d, lo) for d in range(nz // 2, -1, -1) for lo in (3 * H, 2 * H, 0)]

    def run(some):
        for d, lo in some:
            for sc in (si, st):
                for k in sorted({d, (nz - d) % nz}):
                    if k <= sc.ahead or d <= sc.behind:
                        sc.step(k, lo)

    early = 5 if blocks > 2 else 0
    for b in near_first[:0:-1]:
        gradients(b)
    run(steps[:early])
    gradients(near_first[0])
    sums, comm.next = comm.next, small
    for copy in l1:
        copy.wait_recv()
    L2[y] = functools.reduce(jnp.add, [L1[i] for i in range(XN * CORES)])
    l2 = [comm.send(L2.at[y], L2.at[y], ring_y(k), 5) for k in range(1, ny)]
    small, comm.next = comm.next, sums
    run(steps[early:-3])
    sums, comm.next = comm.next, small
    for copy in l2:
        copy.wait_recv()
    L3[z] = functools.reduce(jnp.add, [L2[i] for i in range(ny)])
    l3 = [comm.send(L3.at[z], L3.at[z], ring_z(k), 6) for k in range(1, nz)]
    small, comm.next = comm.next, sums
    run(steps[-3:])
    for copy in l3:
        copy.wait_recv()
    samples = XN * nz * CORES * ny * 2 * H
    loss[0, 0] = jnp.sum(functools.reduce(jnp.add, [L3[i] for i in range(nz)])) / (2.0 * samples)
    si.result(image_grad)
    st.result(text_grad)
    all_sent()
    comm.sent(3, R1t, other)
    comm.sent(7, R1i, other)
    comm.sent(8, R2t.at[1:], other)
    comm.sent(9, R2i.at[1:], other)
    comm.sent(4, L1.at[1:], other)
    comm.sent(5, L2.at[1:], other)
    comm.sent(6, L3.at[1:], other)


def local(image, text):
    nz = lax.axis_size("row") // (XN * CORES)
    ny = lax.axis_size("col")
    E = image.shape[1]
    cols, rws = nz * 2 * G, ny * G
    vmem = lambda *shape, dtype=f32: pltpu.VMEM(shape, dtype)

    def ring(n):
        ahead, behind = n // 2, max(n - 1 - n // 2, 1)
        return [vmem(n, H, E), vmem(ahead, G, E), vmem(behind, G, E), vmem(H, E)]

    scratch = [
        vmem(nz, 2 * G, E),
        vmem(ny, G, E),
        vmem(cols, E, dtype=bf16),
        vmem(cols, E, dtype=bf16),
        vmem(rws, E, dtype=bf16),
        vmem(rws, E, dtype=bf16),
        vmem(rws, cols),
        vmem(rws, cols),
        vmem(rws, cols, dtype=bf16),
        vmem(rws, cols, dtype=bf16),
        vmem(nz, 2 * G, E),
        vmem(nz, G, E),
        vmem(ny, G, E),
        *ring(nz),
        *ring(ny),
        vmem(2, nz, 128),
        vmem(2, ny, 128),
        vmem(3, 2, nz, 128),
        vmem(2, ny, 128),
        vmem(nz, 2, nz, 128),
        vmem(ny, 2, ny, 128),
        vmem(nz, 128),
        vmem(ny, 128),
        vmem(XN * CORES, 8, 128),
        vmem(ny, 8, 128),
        vmem(nz, 8, 128),
        pltpu.SemaphoreType.DMA((10,)),
        pltpu.SemaphoreType.DMA((MESSAGES + SMALL,)),
        pltpu.SemaphoreType.DMA((2, 2)),
    ]
    block = pl.BlockSpec(memory_space=pltpu.VMEM)
    loss, image_grad, text_grad = pl.pallas_call(
        functools.partial(kernel, nz, ny),
        out_shape=(
            jax.ShapeDtypeStruct((1, 1), f32),
            jax.ShapeDtypeStruct(image.shape, f32),
            jax.ShapeDtypeStruct(text.shape, f32),
        ),
        in_specs=[pl.BlockSpec(memory_space=pltpu.HBM)] * 2,
        out_specs=(pl.BlockSpec(memory_space=pltpu.SMEM), block, block),
        scratch_shapes=scratch,
        compiler_params=pltpu.CompilerParams(
            collective_id=0, has_side_effects=True, vmem_limit_bytes=60 * 1024 * 1024
        ),
        name="contrastive",
    )(image, text)
    return loss.reshape(()), grad_scale * image_grad, grad_scale * text_grad


def solution(mesh):
    in_specs = (P(("row", "col"), None), P(("col", "row"), None))
    out_specs = (P(), P(("row", "col"), None), P(("col", "row"), None))
    return jax.shard_map(local, mesh=mesh, in_specs=in_specs, out_specs=out_specs, check_vma=False)
```

```python
import functools
import jax
import jax.numpy as jnp
from jax import lax
from jax.experimental import pallas as pl
from jax.experimental.pallas import tpu as pltpu
from jax.sharding import PartitionSpec as P

logit_scale = 20.0
grad_scale = 0.5 * logit_scale
MESH = pl.DeviceIdType.MESH
XN = 4
CORES = 2
H = 16
TREES = ((0, 0, 1, 2, 3), None, (0, 0, 1, 2, 3), (0, 0, 1, 2, 3))
MESSAGES = 76
ONE, TEXT, IMAGE, SUM1, SUM2, SUM3 = range(MESSAGES, MESSAGES + 6)
G = 4 * H
f32 = jnp.float32
bf16 = jnp.bfloat16
NT = (((1,), (1,)), ((), ()))
NN = (((1,), (0,)), ((), ()))
TN = (((0,), (0,)), ((), ()))


def dot3(a_hi, a_lo, b_hi, b_lo, dims):
    def dot(a, b):
        return lax.dot_general(a, b, dims, preferred_element_type=f32)

    return dot(a_hi, b_hi) + (dot(a_hi, b_lo) + dot(a_lo, b_hi))


def split(value):
    high = value.astype(bf16)
    return high, (value - high.astype(f32)).astype(bf16)


def merge(parts):
    peak = functools.reduce(jnp.maximum, [p for p, _ in parts])
    total = functools.reduce(jnp.add, [t * jnp.exp(p - peak) for p, t in parts])
    return peak, total


class Comm:
    def __init__(self, send_sem, recv_sem):
        self.send_sem, self.recv_sem, self.next = send_sem, recv_sem, 0

    def send(self, src, dst, device, group, shared=None):
        if shared is None:
            shared, self.next = self.next, self.next + 1
        copy = pltpu.make_async_remote_copy(
            src_ref=src,
            dst_ref=dst,
            send_sem=self.send_sem.at[group],
            recv_sem=self.recv_sem.at[shared],
            device_id=device,
            device_id_type=MESH,
        )
        copy.start()
        return copy

    def sent(self, group, like, device):
        pltpu.make_async_remote_copy(
            src_ref=like,
            dst_ref=like,
            send_sem=self.send_sem.at[group],
            recv_sem=self.recv_sem.at[0],
            device_id=device,
            device_id_type=MESH,
        ).wait_send()


    def received(self, shared, like, device):
        pltpu.make_async_remote_copy(
            src_ref=like,
            dst_ref=like,
            send_sem=self.send_sem.at[0],
            recv_sem=self.recv_sem.at[shared],
            device_id=device,
            device_id_type=MESH,
        ).wait_recv()


class Trees:
    def __init__(self, n):
        self.n, self.ahead, self.behind = n, n // 2, n - 1 - n // 2

    def parent(self, lo, d):
        return TREES[lo // H][d]

    def side(self, k):
        return (k, 1, self.ahead) if k <= self.ahead else (self.n - k, -1, self.behind)

    def sides(self, k):
        return [(0, 1, self.ahead), (0, -1, self.behind)] if k == 0 else [self.side(k)]

    def children(self, lo, d, most):
        return [c for c in range(most, d, -1) if self.parent(lo, c) == d]

    def slot(self, d, way):
        return (way * d) % self.n


class Gather(Trees):
    def __init__(self, comm, buf, n, ring, partner, other, group):
        super().__init__(n)
        self.comm, self.buf, self.at, self.partner, self.other, self.group = comm, buf, ring, partner, other, group
        self.cross, self.ring, self.core = {}, {}, {}

    def start(self):
        self.q_cross = self.comm.send(
            self.buf.at[0, 2 * H : 3 * H], self.buf.at[0, 3 * H : G], self.partner, self.group
        )
        self.forward(0, 0)
        self.send_cross(0)
        self.forward(0, 2 * H)

    def start_cross(self):
        self.q_cross.wait_recv()
        self.forward(0, 3 * H)

    def forward(self, k, lo):
        for d, way, most in self.sides(k):
            for c in self.children(lo, d, most):
                to = self.slot(c, way)
                self.ring[to, lo] = self.comm.send(
                    self.buf.at[k, lo : lo + H],
                    self.buf.at[to, lo : lo + H],
                    self.at((-way * (c - d)) % self.n),
                    self.group,
                )

    def send_cross(self, k):
        self.cross[k] = self.comm.send(
            self.buf.at[k, 0:H], self.buf.at[k, H : 2 * H], self.partner, self.group
        )

    def positions(self, s):
        if s > self.ahead:
            return []
        return sorted({s % self.n, (self.n - s) % self.n} if s <= self.behind else {s})

    def step(self, s, lo):
        for k in self.positions(s):
            self.ring[k, lo].wait_recv()
            self.forward(k, lo)
            if lo == 0:
                self.send_cross(k)

    def pass_core(self, k, lo):
        if self.other is not None:
            to = (self.n - k) % self.n
            self.core[to, lo] = self.comm.send(
                self.buf.at[k, lo : lo + 2 * H], self.buf.at[to, G + lo : G + lo + 2 * H], self.other, 1
            )

    def finish_q(self, s):
        for k in self.positions(s):
            self.pass_core(k, 2 * H)

    def finish_p(self, s):
        for k in self.positions(s):
            self.cross[k].wait_recv()
            self.pass_core(k, 0)


class Scatter(Trees):
    def __init__(self, comm, acc, cross_buf, up_buf, down_buf, q_cross, n, ring, partner, group):
        super().__init__(n)
        self.comm, self.acc, self.cross_buf = comm, acc, cross_buf
        self.bufs, self.q_cross_buf = {1: up_buf, -1: down_buf}, q_cross
        self.at, self.partner, self.group = ring, partner, group
        self.cross, self.rings = {}, {}
        self.far = sorted(range(n), key=lambda k: -min(k, n - k))

    def send_cross(self, k):
        self.cross[k] = self.comm.send(
            self.acc.at[k, H : 2 * H], self.cross_buf.at[k], self.partner, self.group
        )

    def leaf(self, k, lo):
        return not any(self.children(lo, d, most) for d, _, most in self.sides(k))

    def launch(self, k, lo):
        d, way, _ = self.side(k)
        dst = self.bufs[way].at[d - 1, lo : lo + H]
        to = self.at((way * (d - self.parent(lo, d))) % self.n)
        copy = self.comm.send(self.acc.at[k, lo : lo + H], dst, to, self.group)
        self.rings[way, d, lo] = (copy, dst)

    def begin(self, ks):
        for k in ks:
            self.send_cross(k)
        for k in ks:
            for lo in (3 * H, 2 * H):
                if self.leaf(k, lo):
                    self.launch(k, lo)

    def step(self, k, lo):
        if lo == 0:
            self.cross[k].wait_recv()
            self.acc[k, 0:H] += self.cross_buf[k]
            if self.leaf(k, lo):
                self.launch(k, lo)
        if self.leaf(k, lo):
            return
        for d, way, most in self.sides(k):
            for c in self.children(lo, d, most):
                copy, dst = self.rings[way, c, lo]
                copy.wait_recv()
                self.acc[k, lo : lo + H] += dst[...]
        if k:
            self.launch(k, lo)
        elif lo == 3 * H:
            self.last = self.comm.send(self.acc.at[0, lo:G], self.q_cross_buf, self.partner, self.group)

    def result(self, out):
        out[0:H] = self.acc[0, 0:H]
        self.last.wait_recv()
        out[H : 2 * H] = self.acc[0, 2 * H : 3 * H] + self.q_cross_buf[...]


def kernel(nz, ny, image, text, loss, image_grad, text_grad,
           T, I, Th, Tl, Ih, Il, L, Er, Wh, Wl, TP, CR, IP,
           tx, tu, td, tq, ix, iu, id_, iq,
           St, Si, R1t, R2t, R2i, Ft, Fi, L1, L2, L3, send_sem, recv_sem, own_sem):
    row, y = lax.axis_index("row"), lax.axis_index("col")
    x, z, c = row // (CORES * nz), (row // CORES) % nz, row % CORES
    turn = 1 - 2 * c
    xt = x + 1 - 2 * (x % 2)
    xi = XN - 1 - x

    def at(x_=x, y_=y, z_=z, c_=c):
        return (x_ * (CORES * nz) + z_ * CORES + c_, y_)

    z_of = [(z + turn * k + nz) % nz for k in range(nz)]
    y_of = [(y + turn * k + ny) % ny for k in range(ny)]
    z_ids, y_ids = [at(z_=v) for v in z_of], [at(y_=v) for v in y_of]
    ring_z, ring_y = z_ids.__getitem__, y_ids.__getitem__
    places = [(x * CORES + c + i) % (XN * CORES) for i in range(XN * CORES)]
    plane = [at(x_=j // CORES, c_=j % CORES) for j in places].__getitem__
    other, at_xt, at_xi = at(c_=1 - c), at(x_=xt), at(x_=xi)
    across_t, across_i = [at(x_=xt, z_=v) for v in z_of], [at(x_=xi, y_=v) for v in y_of]
    cols, rws = nz * 2 * G, ny * G
    comm = Comm(send_sem, recv_sem)

    own_copies = [
        pltpu.make_async_copy(src.at[h * H : (h + 1) * H], dst.at[0, 2 * h * H : (2 * h + 1) * H], own_sem.at[i, h])
        for i, (src, dst) in enumerate(((text, T), (image, I)))
        for h in (1, 0)
    ]
    for copy in own_copies:
        copy.start()
    barrier = pltpu.get_barrier_semaphore()
    peers = [ring_z(k) for k in range(1, nz)] + [ring_y(k) for k in range(1, ny)]
    peers += [plane(i) for i in range(1, XN * CORES)] + across_t[1:] + across_i[1:]
    for peer in peers:
        pl.semaphore_signal(barrier, inc=1, device_id=peer, device_id_type=MESH)
    for copy in own_copies:
        copy.wait()
    pl.semaphore_wait(barrier, len(peers))

    gt = Gather(comm, T, nz, ring_z, at_xt, other, 0)
    gi = Gather(comm, I, ny, ring_y, at_xi, None, 2)
    both = (gt, gi)
    for g in both:
        g.start()
    for g in both:
        g.start_cross()
    def late(s):
        for g in both:
            if s:
                g.step(s, 3 * H)
        for g in both:
            g.finish_q(s)
        for g in both:
            g.finish_p(s)

    last = max(nz, ny) // 2
    for s in range(1, last + 1):
        for lo in (0, 2 * H):
            for g in both:
                g.step(s, lo)
        late(s - 1)

    block = min(256, cols)
    blocks = cols // block
    per = block // 128
    half = ny // 2
    distance = lambda k, n: min(k, n - k)
    near_first = sorted(range(blocks), key=lambda b: max(distance(k, nz) for k in range(b * per, (b + 1) * per)))

    def take_image(h):
        for k in range(h * half, (h + 1) * half):
            Ih[k * G : (k + 1) * G], Il[k * G : (k + 1) * G] = split(I[k])

    def take_text(b):
        for k in range(b * per, (b + 1) * per):
            gt.core[k, 0].wait_recv()
            gt.core[k, 2 * H].wait_recv()
            first = k * 2 * G
            Th[first : first + 2 * G], Tl[first : first + 2 * G] = split(T[k])

    def logits(rows, b):
        span = slice(b * block, (b + 1) * block)
        L[rows, span] = logit_scale * dot3(Ih[rows], Il[rows], Th[span], Tl[span], NT)

    low, high = slice(0, half * G), slice(half * G, rws)
    take_image(0)
    for b in near_first[:-2]:
        take_text(b)
        logits(low, b)
    late(last)
    for b in near_first[:-1][-1:]:
        take_text(b)
        logits(low, b)
    take_image(1)
    for b in near_first[:-1]:
        logits(high, b)
    take_text(near_first[-1])
    logits(slice(0, rws), near_first[-1])

    def all_sent():
        comm.sent(0, T.at[0 : nz // 2, 0 : 2 * G - G // nz], other)
        comm.sent(1, T.at[0 : nz // 2], other)
        comm.sent(2, T.at[0 : ny // 2, 0 : 2 * G - G // ny], other)

    all_sent()
    def iota(shape, dim):
        return lax.broadcasted_iota(jnp.int32, shape, dim)

    lane = iota((1, cols), 1)
    at_z = (z + turn * (lane >> 7) + nz) & (nz - 1)
    at_x = jnp.where((lane >> 4) & 1 == 0, x, xt)
    at_c = jnp.where((lane >> 6) & 1 == 0, c, 1 - c)
    col_ids = (
        y * (XN * nz * CORES * 2 * H)
        + ((at_x * nz + at_z) * CORES + at_c) * (2 * H)
        + ((lane >> 5) & 1) * H
        + (lane & 15)
    )

    def row_ids(k):
        r = iota((G, 1), 0)
        of_x = jnp.where((r >> 4) & 1 == 0, x, xi)
        of_y = (y + turn * k + ny) & (ny - 1)
        return ((of_x * nz + z) * CORES + c) * (ny * 2 * H) + of_y * (2 * H) + ((r >> 5) & 1) * H + (r & 15)

    own_lane = iota((G, 128), 0) == iota((G, 128), 1)

    def to_lanes(column):
        return jnp.sum(jnp.where(own_lane, column, 0.0), axis=0, keepdims=True)

    def to_column(lanes):
        return jnp.sum(jnp.where(own_lane, lanes, 0.0), axis=1, keepdims=True)

    def group8(v, op):
        return op(v.reshape(v.shape[0] // 8, 8, v.shape[1]), axis=0)

    def share(buf, ids, n, group, shared):
        for p, ring in enumerate(ids):
            for k in range(1 - p, n):
                comm.send(buf.at[0], buf.at[p * n + (n - k) % n], ring[k], group, shared)

    def row_pass(k, carry):
        peak, diag = carry
        here = pl.ds(pl.multiple_of(k * G, G), G)
        tile = L[here]
        row_peak = jnp.max(tile, axis=1, keepdims=True)
        terms = jnp.exp(tile - row_peak)
        Er[here] = terms
        Si[0, pl.ds(k, 1)] = to_lanes(row_peak)
        Si[1, pl.ds(k, 1)] = to_lanes(jnp.sum(terms, axis=1, keepdims=True))
        diag = diag + group8(jnp.where(row_ids(k) == col_ids, tile, 0.0), jnp.sum)
        return jnp.maximum(peak, group8(tile, jnp.max)), diag

    start = (jnp.full((8, cols), -jnp.inf, f32), jnp.zeros((8, cols), f32))
    peak8, diag8 = lax.fori_loop(0, ny, row_pass, start)
    col_peak = jnp.max(peak8, axis=0, keepdims=True)
    valid = iota((ny, 128), 1) < G
    R2i[0] = jnp.where(valid, Si[0], pltpu.roll(Si[1], G, 1))
    share(R2i, [y_ids, across_i], ny, 8, IMAGE)
    lanes_n = cols // 128
    diag_sum = functools.reduce(jnp.add, [diag8[:, i * 128 : (i + 1) * 128] for i in range(lanes_n)])

    def col_pass(k, total):
        here = pl.ds(pl.multiple_of(k * G, G), G)
        terms = jnp.exp(L[here] - col_peak)
        L[here] = terms
        return total + group8(terms, jnp.sum)

    col_total = jnp.sum(lax.fori_loop(0, ny, col_pass, jnp.zeros((8, cols), f32)), axis=0, keepdims=True)

    def fold(v):
        return jnp.concatenate([v[:, k * 128 : (k + 1) * 128] for k in range(nz)], axis=0)

    St[0], St[1] = fold(col_peak), fold(col_total)

    comm.send(St, R1t, other, 3, ONE)

    def swap_x(v):
        low = (iota(v.shape, 1) >> 4) & 1 == 0
        return jnp.where(low, pltpu.roll(v, 128 - H, 1), pltpu.roll(v, H, 1))

    def swap_core(v):
        v = pltpu.roll(v, G, 1)
        return jnp.concatenate([v[(nz - k) % nz : (nz - k) % nz + 1] for k in range(nz)], axis=0)

    def shift(v, k, n):
        return jnp.concatenate([v[n - k :], v[: n - k]], axis=0)

    def ring_of(buf, n):
        for p in range(2):
            for k in range(n):
                v = swap_x(buf[p * n + k]) if p else buf[k]
                yield shift(v, k, n) if k else v

    peak_t, peak_i = St[0], Si[0]
    comm.received(ONE, R1t, other)
    pt, tt = merge([(peak_t, St[1]), (swap_core(R1t[0]), swap_core(R1t[1]))])
    R2t[0] = pt + jnp.log(tt)
    share(R2t, [z_ids, across_t], nz, 7, TEXT)
    comm.received(IMAGE, R2i.at[1:], other)
    pi, ti = merge([
        (jnp.where(valid, v, 0.0), jnp.where(valid, pltpu.roll(v, G, 1), 1.0)) for v in ring_of(R2i, ny)
    ])
    comm.received(TEXT, R2t.at[1:], other)
    pt, tt = merge([(v, 1.0) for v in ring_of(R2t, nz)])
    Ft[...] = jnp.exp(peak_t - pt) / tt
    Fi[...] = jnp.exp(peak_i - pi) / ti

    def own(v):
        i = iota(v.shape, 1)
        mine = (iota(v.shape, 0) == 0) & (i < G) & ((i >> 4) & 1 == 0)
        return jnp.sum(jnp.where(mine, v, 0.0), axis=0, keepdims=True)

    first = iota((8, 128), 0) == 0
    part = own(pt + jnp.log(tt)) + own(pi + jnp.log(ti))
    L1[x * CORES + c] = jnp.where(first, part, 0.0) - 2.0 * diag_sum
    for i in range(1, XN * CORES):
        comm.send(L1.at[x * CORES + c], L1.at[x * CORES + c], plane(i), 4, SUM1)

    col_factor = jnp.concatenate([Ft[k : k + 1] for k in range(nz)], axis=1)

    def weigh(k, _):
        here = pl.ds(pl.multiple_of(k * G, G), G)
        value = Er[here] * to_column(Fi[pl.ds(k, 1)]) + L[here] * col_factor
        value = value - jnp.where(row_ids(k) == col_ids, 2.0, 0.0)
        Wh[here], Wl[here] = split(value)
        return 0

    lax.fori_loop(0, ny, weigh, 0)

    comm.next = 0
    st = Scatter(comm, TP, tx, tu, td, tq, nz, ring_z, at_xt, 0)
    si = Scatter(comm, IP, ix, iu, id_, iq, ny, ring_y, at_xi, 2)
    core, done, added = {}, [], []

    def gradients(b):
        span = slice(b * block, (b + 1) * block)
        part = dot3(Wh[:, span], Wl[:, span], Ih[...], Il[...], TN)
        here = list(range(b * per, (b + 1) * per))
        for i, k in enumerate(here):
            TP[k] = part[i * 128 : (i + 1) * 128]
            to = (nz - k) % nz
            core[to] = comm.send(TP.at[k, G : 2 * G], CR.at[to], other, 1)
        rows = slice(here[0] * G, (here[-1] + 1) * G)
        part = dot3(Wh[rows], Wl[rows], Th[...], Tl[...], NN)
        for i, k in enumerate(here):
            IP[k] = part[i * G : (i + 1) * G]
        si.begin([k for k in si.far if k in here])
        done.extend(here)
        ready = [k for k in st.far if k in done and (nz - k) % nz in done and k not in added]
        for k in ready:
            core[k].wait_recv()
            TP[k, 0:G] += CR[k]
        added.extend(ready)
        st.begin(ready)

    steps = [(d, lo) for d in range(nz // 2, -1, -1) for lo in (3 * H, 2 * H, 0)]

    def run(some):
        for d, lo in some:
            for sc in (si, st):
                for k in sorted({d, (nz - d) % nz}):
                    if k <= sc.ahead or d <= sc.behind:
                        sc.step(k, lo)

    early = 5 if blocks > 2 else 0
    for b in near_first[:0:-1]:
        gradients(b)
    comm.received(SUM1, L1.at[1:], other)
    L2[y] = functools.reduce(jnp.add, [L1[i] for i in range(XN * CORES)])
    for k in range(1, ny):
        comm.send(L2.at[y], L2.at[y], ring_y(k), 5, SUM2)
    run(steps[:early])
    gradients(near_first[0])
    run(steps[early : early + 1])
    comm.received(SUM2, L2.at[1:], other)
    L3[z] = functools.reduce(jnp.add, [L2[i] for i in range(ny)])
    for k in range(1, nz):
        comm.send(L3.at[z], L3.at[z], ring_z(k), 6, SUM3)
    run(steps[early + 1 : -3])
    comm.received(SUM3, L3.at[1:], other)
    samples = XN * nz * CORES * ny * 2 * H
    loss[0, 0] = jnp.sum(functools.reduce(jnp.add, [L3[i] for i in range(nz)])) / (2.0 * samples)
    run(steps[-3:])
    si.result(image_grad)
    st.result(text_grad)
    all_sent()
    comm.sent(3, R1t, other)
    comm.sent(7, R2t.at[1:], other)
    comm.sent(8, R2i.at[1:], other)
    comm.sent(4, L1.at[1:], other)
    comm.sent(5, L2.at[1:], other)
    comm.sent(6, L3.at[1:], other)


def local(image, text):
    nz = lax.axis_size("row") // (XN * CORES)
    ny = lax.axis_size("col")
    E = image.shape[1]
    cols, rws = nz * 2 * G, ny * G
    vmem = lambda *shape, dtype=f32: pltpu.VMEM(shape, dtype)

    def ring(n):
        ahead, behind = n // 2, max(n - 1 - n // 2, 1)
        return [vmem(n, H, E), vmem(ahead, G, E), vmem(behind, G, E), vmem(H, E)]

    scratch = [
        vmem(nz, 2 * G, E),
        vmem(ny, G, E),
        vmem(cols, E, dtype=bf16),
        vmem(cols, E, dtype=bf16),
        vmem(rws, E, dtype=bf16),
        vmem(rws, E, dtype=bf16),
        vmem(rws, cols),
        vmem(rws, cols),
        vmem(rws, cols, dtype=bf16),
        vmem(rws, cols, dtype=bf16),
        vmem(nz, 2 * G, E),
        vmem(nz, G, E),
        vmem(ny, G, E),
        *ring(nz),
        *ring(ny),
        vmem(2, nz, 128),
        vmem(2, ny, 128),
        vmem(2, nz, 128),
        vmem(2 * nz, nz, 128),
        vmem(2 * ny, ny, 128),
        vmem(nz, 128),
        vmem(ny, 128),
        vmem(XN * CORES, 8, 128),
        vmem(ny, 8, 128),
        vmem(nz, 8, 128),
        pltpu.SemaphoreType.DMA((9,)),
        pltpu.SemaphoreType.DMA((MESSAGES + 6,)),
        pltpu.SemaphoreType.DMA((2, 2)),
    ]
    block = pl.BlockSpec(memory_space=pltpu.VMEM)
    loss, image_grad, text_grad = pl.pallas_call(
        functools.partial(kernel, nz, ny),
        out_shape=(
            jax.ShapeDtypeStruct((1, 1), f32),
            jax.ShapeDtypeStruct(image.shape, f32),
            jax.ShapeDtypeStruct(text.shape, f32),
        ),
        in_specs=[pl.BlockSpec(memory_space=pltpu.HBM)] * 2,
        out_specs=(pl.BlockSpec(memory_space=pltpu.SMEM), block, block),
        scratch_shapes=scratch,
        compiler_params=pltpu.CompilerParams(
            collective_id=0, has_side_effects=True, vmem_limit_bytes=60 * 1024 * 1024
        ),
        name="contrastive",
    )(image, text)
    return loss.reshape(()), grad_scale * image_grad, grad_scale * text_grad


def solution(mesh):
    in_specs = (P(("row", "col"), None), P(("col", "row"), None))
    out_specs = (P(), P(("row", "col"), None), P(("col", "row"), None))
    return jax.shard_map(local, mesh=mesh, in_specs=in_specs, out_specs=out_specs, check_vma=False)
```

```python
import functools
import jax
import jax.numpy as jnp
from jax import lax
from jax.experimental import pallas as pl
from jax.experimental.pallas import tpu as pltpu
from jax.sharding import PartitionSpec as P

logit_scale = 20.0
grad_scale = 0.5 * logit_scale
MESH = pl.DeviceIdType.MESH
XN = 4
CORES = 2
H = 16
TREES = ((0, 0, 1, 2, 3), None, (0, 0, 1, 2, 3), (0, 0, 1, 2, 3))
MESSAGES = 76
ONE, TEXT, IMAGE, SUM1, SUM2, SUM3 = range(MESSAGES, MESSAGES + 6)
G = 4 * H
f32 = jnp.float32
bf16 = jnp.bfloat16
NT = (((1,), (1,)), ((), ()))
NN = (((1,), (0,)), ((), ()))
TN = (((0,), (0,)), ((), ()))


def dot3(a_hi, a_lo, b_hi, b_lo, dims):
    def dot(a, b):
        return lax.dot_general(a, b, dims, preferred_element_type=f32)

    return dot(a_hi, b_hi) + (dot(a_hi, b_lo) + dot(a_lo, b_hi))


def split(value):
    high = value.astype(bf16)
    return high, (value - high.astype(f32)).astype(bf16)


def merge(parts):
    peak = functools.reduce(jnp.maximum, [p for p, _ in parts])
    total = functools.reduce(jnp.add, [t * jnp.exp(p - peak) for p, t in parts])
    return peak, total


class Comm:
    def __init__(self, send_sem, recv_sem):
        self.send_sem, self.recv_sem, self.next = send_sem, recv_sem, 0

    def send(self, src, dst, device, group, shared=None):
        if shared is None:
            shared, self.next = self.next, self.next + 1
        copy = pltpu.make_async_remote_copy(
            src_ref=src,
            dst_ref=dst,
            send_sem=self.send_sem.at[group],
            recv_sem=self.recv_sem.at[shared],
            device_id=device,
            device_id_type=MESH,
        )
        copy.start()
        return copy

    def sent(self, group, like, device):
        pltpu.make_async_remote_copy(
            src_ref=like,
            dst_ref=like,
            send_sem=self.send_sem.at[group],
            recv_sem=self.recv_sem.at[0],
            device_id=device,
            device_id_type=MESH,
        ).wait_send()


    def received(self, shared, like, device):
        pltpu.make_async_remote_copy(
            src_ref=like,
            dst_ref=like,
            send_sem=self.send_sem.at[0],
            recv_sem=self.recv_sem.at[shared],
            device_id=device,
            device_id_type=MESH,
        ).wait_recv()


class Trees:
    def __init__(self, n):
        self.n, self.ahead, self.behind = n, n // 2, n - 1 - n // 2

    def parent(self, lo, d):
        return TREES[lo // H][d]

    def side(self, k):
        return (k, 1, self.ahead) if k <= self.ahead else (self.n - k, -1, self.behind)

    def sides(self, k):
        return [(0, 1, self.ahead), (0, -1, self.behind)] if k == 0 else [self.side(k)]

    def children(self, lo, d, most):
        return [c for c in range(most, d, -1) if self.parent(lo, c) == d]

    def slot(self, d, way):
        return (way * d) % self.n


class Gather(Trees):
    def __init__(self, comm, buf, n, ring, partner, other, group):
        super().__init__(n)
        self.comm, self.buf, self.at, self.partner, self.other, self.group = comm, buf, ring, partner, other, group
        self.cross, self.ring, self.core = {}, {}, {}

    def start(self):
        self.q_cross = self.comm.send(
            self.buf.at[0, 2 * H : 3 * H], self.buf.at[0, 3 * H : G], self.partner, self.group
        )
        self.forward(0, 0)
        self.send_cross(0)
        self.forward(0, 2 * H)

    def start_cross(self):
        self.q_cross.wait_recv()
        self.forward(0, 3 * H)

    def forward(self, k, lo):
        for d, way, most in self.sides(k):
            for c in self.children(lo, d, most):
                to = self.slot(c, way)
                self.ring[to, lo] = self.comm.send(
                    self.buf.at[k, lo : lo + H],
                    self.buf.at[to, lo : lo + H],
                    self.at((-way * (c - d)) % self.n),
                    self.group,
                )

    def send_cross(self, k):
        self.cross[k] = self.comm.send(
            self.buf.at[k, 0:H], self.buf.at[k, H : 2 * H], self.partner, self.group
        )

    def positions(self, s):
        if s > self.ahead:
            return []
        return sorted({s % self.n, (self.n - s) % self.n} if s <= self.behind else {s})

    def step(self, s, lo):
        for k in self.positions(s):
            self.ring[k, lo].wait_recv()
            self.forward(k, lo)
            if lo == 0:
                self.send_cross(k)

    def pass_core(self, k, lo):
        if self.other is not None:
            to = (self.n - k) % self.n
            self.core[to, lo] = self.comm.send(
                self.buf.at[k, lo : lo + 2 * H], self.buf.at[to, G + lo : G + lo + 2 * H], self.other, 1
            )

    def finish_q(self, s):
        for k in self.positions(s):
            self.pass_core(k, 2 * H)

    def finish_p(self, s):
        for k in self.positions(s):
            self.cross[k].wait_recv()
            self.pass_core(k, 0)


class Scatter(Trees):
    def __init__(self, comm, acc, cross_buf, up_buf, down_buf, q_cross, n, ring, partner, group):
        super().__init__(n)
        self.comm, self.acc, self.cross_buf = comm, acc, cross_buf
        self.bufs, self.q_cross_buf = {1: up_buf, -1: down_buf}, q_cross
        self.at, self.partner, self.group = ring, partner, group
        self.cross, self.rings = {}, {}
        self.far = sorted(range(n), key=lambda k: -min(k, n - k))

    def send_cross(self, k):
        self.cross[k] = self.comm.send(
            self.acc.at[k, H : 2 * H], self.cross_buf.at[k], self.partner, self.group
        )

    def leaf(self, k, lo):
        return not any(self.children(lo, d, most) for d, _, most in self.sides(k))

    def launch(self, k, lo):
        d, way, _ = self.side(k)
        dst = self.bufs[way].at[d - 1, lo : lo + H]
        to = self.at((way * (d - self.parent(lo, d))) % self.n)
        copy = self.comm.send(self.acc.at[k, lo : lo + H], dst, to, self.group)
        self.rings[way, d, lo] = (copy, dst)

    def begin(self, ks):
        for k in ks:
            self.send_cross(k)
        for k in ks:
            for lo in (3 * H, 2 * H):
                if self.leaf(k, lo):
                    self.launch(k, lo)

    def step(self, k, lo):
        if lo == 0:
            self.cross[k].wait_recv()
            self.acc[k, 0:H] += self.cross_buf[k]
            if self.leaf(k, lo):
                self.launch(k, lo)
        if self.leaf(k, lo):
            return
        for d, way, most in self.sides(k):
            for c in self.children(lo, d, most):
                copy, dst = self.rings[way, c, lo]
                copy.wait_recv()
                self.acc[k, lo : lo + H] += dst[...]
        if k:
            self.launch(k, lo)
        elif lo == 3 * H:
            self.last = self.comm.send(self.acc.at[0, lo:G], self.q_cross_buf, self.partner, self.group)

    def result(self, out):
        out[0:H] = self.acc[0, 0:H]
        self.last.wait_recv()
        out[H : 2 * H] = self.acc[0, 2 * H : 3 * H] + self.q_cross_buf[...]


def kernel(nz, ny, image, text, loss, image_grad, text_grad,
           T, I, Th, Tl, Ih, Il, L, Er, Wh, Wl, TP, CR, IP,
           tx, tu, td, tq, ix, iu, id_, iq,
           St, Si, R1t, R2t, R2i, Ft, Fi, L1, L2, L3, send_sem, recv_sem, own_sem):
    row, y = lax.axis_index("row"), lax.axis_index("col")
    x, z, c = row // (CORES * nz), (row // CORES) % nz, row % CORES
    turn = 1 - 2 * c
    xt = x + 1 - 2 * (x % 2)
    xi = XN - 1 - x

    def at(x_=x, y_=y, z_=z, c_=c):
        return (x_ * (CORES * nz) + z_ * CORES + c_, y_)

    z_of = [(z + turn * k + nz) % nz for k in range(nz)]
    y_of = [(y + turn * k + ny) % ny for k in range(ny)]
    z_ids, y_ids = [at(z_=v) for v in z_of], [at(y_=v) for v in y_of]
    ring_z, ring_y = z_ids.__getitem__, y_ids.__getitem__
    places = [(x * CORES + c + i) % (XN * CORES) for i in range(XN * CORES)]
    plane = [at(x_=j // CORES, c_=j % CORES) for j in places].__getitem__
    other, at_xt, at_xi = at(c_=1 - c), at(x_=xt), at(x_=xi)
    across_t, across_i = [at(x_=xt, z_=v) for v in z_of], [at(x_=xi, y_=v) for v in y_of]
    cols, rws = nz * 2 * G, ny * G
    comm = Comm(send_sem, recv_sem)

    own_copies = [
        pltpu.make_async_copy(src.at[h * H : (h + 1) * H], dst.at[0, 2 * h * H : (2 * h + 1) * H], own_sem.at[i, h])
        for i, (src, dst) in enumerate(((text, T), (image, I)))
        for h in (1, 0)
    ]
    for copy in own_copies:
        copy.start()
    barrier = pltpu.get_barrier_semaphore()
    peers = [ring_z(k) for k in range(1, nz)] + [ring_y(k) for k in range(1, ny)]
    peers += [plane(i) for i in range(1, XN * CORES)] + across_t[1:] + across_i[1:]
    for peer in peers:
        pl.semaphore_signal(barrier, inc=1, device_id=peer, device_id_type=MESH)
    for copy in own_copies:
        copy.wait()
    pl.semaphore_wait(barrier, len(peers))

    gt = Gather(comm, T, nz, ring_z, at_xt, other, 0)
    gi = Gather(comm, I, ny, ring_y, at_xi, None, 2)
    both = (gt, gi)
    for g in both:
        g.start()
    for g in both:
        g.start_cross()
    def late(s):
        for g in both:
            if s:
                g.step(s, 3 * H)
        for g in both:
            g.finish_q(s)
        for g in both:
            g.finish_p(s)

    last = max(nz, ny) // 2
    for s in range(1, last + 1):
        for lo in (0, 2 * H):
            for g in both:
                g.step(s, lo)
        late(s - 1)

    block = min(256, cols)
    blocks = cols // block
    per = block // 128
    half = ny // 2
    distance = lambda k, n: min(k, n - k)
    near_first = sorted(range(blocks), key=lambda b: max(distance(k, nz) for k in range(b * per, (b + 1) * per)))

    def take_image(h):
        for k in range(h * half, (h + 1) * half):
            Ih[k * G : (k + 1) * G], Il[k * G : (k + 1) * G] = split(I[k])

    def take_text(b):
        for k in range(b * per, (b + 1) * per):
            gt.core[k, 0].wait_recv()
            gt.core[k, 2 * H].wait_recv()
            first = k * 2 * G
            Th[first : first + 2 * G], Tl[first : first + 2 * G] = split(T[k])

    def logits(rows, b):
        span = slice(b * block, (b + 1) * block)
        L[rows, span] = logit_scale * dot3(Ih[rows], Il[rows], Th[span], Tl[span], NT)

    low, high = slice(0, half * G), slice(half * G, rws)
    take_image(0)
    for b in near_first[:-2]:
        take_text(b)
        logits(low, b)
    late(last)
    for b in near_first[:-1][-1:]:
        take_text(b)
        logits(low, b)
    take_image(1)
    for b in near_first[:-1]:
        logits(high, b)
    take_text(near_first[-1])
    logits(slice(0, rws), near_first[-1])

    def all_sent():
        comm.sent(0, T.at[0 : nz // 2, 0 : 2 * G - G // nz], other)
        comm.sent(1, T.at[0 : nz // 2], other)
        comm.sent(2, T.at[0 : ny // 2, 0 : 2 * G - G // ny], other)

    all_sent()
    def iota(shape, dim):
        return lax.broadcasted_iota(jnp.int32, shape, dim)

    lane = iota((1, cols), 1)
    at_z = (z + turn * (lane >> 7) + nz) & (nz - 1)
    at_x = jnp.where((lane >> 4) & 1 == 0, x, xt)
    at_c = jnp.where((lane >> 6) & 1 == 0, c, 1 - c)
    col_ids = (
        y * (XN * nz * CORES * 2 * H)
        + ((at_x * nz + at_z) * CORES + at_c) * (2 * H)
        + ((lane >> 5) & 1) * H
        + (lane & 15)
    )

    def row_ids(k):
        r = iota((G, 1), 0)
        of_x = jnp.where((r >> 4) & 1 == 0, x, xi)
        of_y = (y + turn * k + ny) & (ny - 1)
        return ((of_x * nz + z) * CORES + c) * (ny * 2 * H) + of_y * (2 * H) + ((r >> 5) & 1) * H + (r & 15)

    own_lane = iota((G, 128), 0) == iota((G, 128), 1)

    def to_lanes(column):
        return jnp.sum(jnp.where(own_lane, column, 0.0), axis=0, keepdims=True)

    def to_column(lanes):
        return jnp.sum(jnp.where(own_lane, lanes, 0.0), axis=1, keepdims=True)

    def group8(v, op):
        return op(v.reshape(v.shape[0] // 8, 8, v.shape[1]), axis=0)

    def share(buf, ids, n, group, shared):
        for p, ring in enumerate(ids):
            for k in range(1 - p, n):
                comm.send(buf.at[0], buf.at[p * n + (n - k) % n], ring[k], group, shared)

    def row_pass(k, carry):
        peak, diag = carry
        here = pl.ds(pl.multiple_of(k * G, G), G)
        tile = L[here]
        row_peak = jnp.max(tile, axis=1, keepdims=True)
        terms = jnp.exp(tile - row_peak)
        Er[here] = terms
        Si[0, pl.ds(k, 1)] = to_lanes(row_peak)
        Si[1, pl.ds(k, 1)] = to_lanes(jnp.sum(terms, axis=1, keepdims=True))
        diag = diag + group8(jnp.where(row_ids(k) == col_ids, tile, 0.0), jnp.sum)
        return jnp.maximum(peak, group8(tile, jnp.max)), diag

    start = (jnp.full((8, cols), -jnp.inf, f32), jnp.zeros((8, cols), f32))
    peak8, diag8 = lax.fori_loop(0, ny, row_pass, start)
    col_peak = jnp.max(peak8, axis=0, keepdims=True)
    valid = iota((ny, 128), 1) < G
    R2i[0] = jnp.where(valid, Si[0], pltpu.roll(Si[1], G, 1))
    share(R2i, [y_ids, across_i], ny, 8, IMAGE)
    lanes_n = cols // 128
    diag_sum = functools.reduce(jnp.add, [diag8[:, i * 128 : (i + 1) * 128] for i in range(lanes_n)])

    def col_pass(k, total):
        here = pl.ds(pl.multiple_of(k * G, G), G)
        terms = jnp.exp(L[here] - col_peak)
        L[here] = terms
        return total + group8(terms, jnp.sum)

    col_total = jnp.sum(lax.fori_loop(0, ny, col_pass, jnp.zeros((8, cols), f32)), axis=0, keepdims=True)

    def fold(v):
        return jnp.concatenate([v[:, k * 128 : (k + 1) * 128] for k in range(nz)], axis=0)

    St[0], St[1] = fold(col_peak), fold(col_total)

    comm.send(St, R1t, other, 3, ONE)

    def swap_x(v):
        low = (iota(v.shape, 1) >> 4) & 1 == 0
        return jnp.where(low, pltpu.roll(v, 128 - H, 1), pltpu.roll(v, H, 1))

    def swap_core(v):
        v = pltpu.roll(v, G, 1)
        return jnp.concatenate([v[(nz - k) % nz : (nz - k) % nz + 1] for k in range(nz)], axis=0)

    def shift(v, k, n):
        return jnp.concatenate([v[n - k :], v[: n - k]], axis=0)

    def ring_of(buf, n):
        for p in range(2):
            for k in range(n):
                v = swap_x(buf[p * n + k]) if p else buf[k]
                yield shift(v, k, n) if k else v

    peak_t, peak_i = St[0], Si[0]
    comm.received(ONE, R1t, other)
    pt, tt = merge([(peak_t, St[1]), (swap_core(R1t[0]), swap_core(R1t[1]))])
    R2t[0] = pt + jnp.log(tt)
    share(R2t, [z_ids, across_t], nz, 7, TEXT)
    comm.received(IMAGE, R2i.at[1:], other)
    pi, ti = merge([
        (jnp.where(valid, v, 0.0), jnp.where(valid, pltpu.roll(v, G, 1), 1.0)) for v in ring_of(R2i, ny)
    ])
    comm.received(TEXT, R2t.at[1:], other)
    pt, tt = merge([(v, 1.0) for v in ring_of(R2t, nz)])
    Ft[...] = jnp.exp(peak_t - pt) / tt
    Fi[...] = jnp.exp(peak_i - pi) / ti

    def own(v):
        i = iota(v.shape, 1)
        mine = (iota(v.shape, 0) == 0) & (i < G) & ((i >> 4) & 1 == 0)
        return jnp.sum(jnp.where(mine, v, 0.0), axis=0, keepdims=True)

    first = iota((8, 128), 0) == 0
    part = own(pt + jnp.log(tt)) + own(pi + jnp.log(ti))
    L1[x * CORES + c] = jnp.where(first, part, 0.0) - 2.0 * diag_sum
    for i in range(1, XN * CORES):
        comm.send(L1.at[x * CORES + c], L1.at[x * CORES + c], plane(i), 4, SUM1)

    col_factor = jnp.concatenate([Ft[k : k + 1] for k in range(nz)], axis=1)

    def weigh(k, _):
        here = pl.ds(pl.multiple_of(k * G, G), G)
        value = Er[here] * to_column(Fi[pl.ds(k, 1)]) + L[here] * col_factor
        value = value - jnp.where(row_ids(k) == col_ids, 2.0, 0.0)
        Wh[here], Wl[here] = split(value)
        return 0

    lax.fori_loop(0, ny, weigh, 0)

    comm.next = 0
    st = Scatter(comm, TP, tx, tu, td, tq, nz, ring_z, at_xt, 0)
    si = Scatter(comm, IP, ix, iu, id_, iq, ny, ring_y, at_xi, 2)
    core, done, added, pending = {}, [], [], []

    def add_core():
        for k in pending:
            core[k].wait_recv()
            TP[k, 0:G] += CR[k]
        st.begin(pending)
        added.extend(pending)
        pending.clear()

    def gradients(b, image_positions):
        span = slice(b * block, (b + 1) * block)
        part = dot3(Wh[:, span], Wl[:, span], Ih[...], Il[...], TN)
        here = list(range(b * per, (b + 1) * per))
        for i, k in enumerate(here):
            TP[k] = part[i * 128 : (i + 1) * 128]
            to = (nz - k) % nz
            core[to] = comm.send(TP.at[k, G : 2 * G], CR.at[to], other, 1)
        add_core()
        if image_positions:
            rows = slice(image_positions[0] * G, (image_positions[-1] + 1) * G)
            part = dot3(Wh[rows], Wl[rows], Th[...], Tl[...], NN)
            for i, k in enumerate(image_positions):
                IP[k] = part[i * G : (i + 1) * G]
            si.begin([k for k in si.far if k in image_positions])
        done.extend(here)
        pending.extend(k for k in st.far if k in done and (nz - k) % nz in done and k not in added)

    steps = [(d, lo) for d in range(nz // 2, -1, -1) for lo in (3 * H, 2 * H, 0)]

    def run(some):
        for d, lo in some:
            for sc in (si, st):
                for k in sorted({d, (nz - d) % nz}):
                    if k <= sc.ahead or d <= sc.behind:
                        sc.step(k, lo)

    early = 5 if blocks > 2 else 0
    shares = {0: range(half, ny), max(blocks - 3, 1): range(half)} if blocks > 1 else {0: range(ny)}
    for i, b in enumerate(near_first[:0:-1]):
        gradients(b, shares.get(i))
    run(steps[:early])
    comm.received(SUM1, L1.at[1:], other)
    L2[y] = functools.reduce(jnp.add, [L1[i] for i in range(XN * CORES)])
    for k in range(1, ny):
        comm.send(L2.at[y], L2.at[y], ring_y(k), 5, SUM2)
    gradients(near_first[0], shares.get(blocks - 1))
    run(steps[early : early + 1])
    add_core()
    run(steps[early + 1 : early + 3])
    comm.received(SUM2, L2.at[1:], other)
    L3[z] = functools.reduce(jnp.add, [L2[i] for i in range(ny)])
    for k in range(1, nz):
        comm.send(L3.at[z], L3.at[z], ring_z(k), 6, SUM3)
    run(steps[early + 3 : -1])
    comm.received(SUM3, L3.at[1:], other)
    samples = XN * nz * CORES * ny * 2 * H
    loss[0, 0] = jnp.sum(functools.reduce(jnp.add, [L3[i] for i in range(nz)])) / (2.0 * samples)
    run(steps[-1:])
    si.result(image_grad)
    st.result(text_grad)
    all_sent()
    comm.sent(3, R1t, other)
    comm.sent(7, R2t.at[1:], other)
    comm.sent(8, R2i.at[1:], other)
    comm.sent(4, L1.at[1:], other)
    comm.sent(5, L2.at[1:], other)
    comm.sent(6, L3.at[1:], other)


def local(image, text):
    nz = lax.axis_size("row") // (XN * CORES)
    ny = lax.axis_size("col")
    E = image.shape[1]
    cols, rws = nz * 2 * G, ny * G
    vmem = lambda *shape, dtype=f32: pltpu.VMEM(shape, dtype)

    def ring(n):
        ahead, behind = n // 2, max(n - 1 - n // 2, 1)
        return [vmem(n, H, E), vmem(ahead, G, E), vmem(behind, G, E), vmem(H, E)]

    scratch = [
        vmem(nz, 2 * G, E),
        vmem(ny, G, E),
        vmem(cols, E, dtype=bf16),
        vmem(cols, E, dtype=bf16),
        vmem(rws, E, dtype=bf16),
        vmem(rws, E, dtype=bf16),
        vmem(rws, cols),
        vmem(rws, cols),
        vmem(rws, cols, dtype=bf16),
        vmem(rws, cols, dtype=bf16),
        vmem(nz, 2 * G, E),
        vmem(nz, G, E),
        vmem(ny, G, E),
        *ring(nz),
        *ring(ny),
        vmem(2, nz, 128),
        vmem(2, ny, 128),
        vmem(2, nz, 128),
        vmem(2 * nz, nz, 128),
        vmem(2 * ny, ny, 128),
        vmem(nz, 128),
        vmem(ny, 128),
        vmem(XN * CORES, 8, 128),
        vmem(ny, 8, 128),
        vmem(nz, 8, 128),
        pltpu.SemaphoreType.DMA((9,)),
        pltpu.SemaphoreType.DMA((MESSAGES + 6,)),
        pltpu.SemaphoreType.DMA((2, 2)),
    ]
    block = pl.BlockSpec(memory_space=pltpu.VMEM)
    loss, image_grad, text_grad = pl.pallas_call(
        functools.partial(kernel, nz, ny),
        out_shape=(
            jax.ShapeDtypeStruct((1, 1), f32),
            jax.ShapeDtypeStruct(image.shape, f32),
            jax.ShapeDtypeStruct(text.shape, f32),
        ),
        in_specs=[pl.BlockSpec(memory_space=pltpu.HBM)] * 2,
        out_specs=(pl.BlockSpec(memory_space=pltpu.SMEM), block, block),
        scratch_shapes=scratch,
        compiler_params=pltpu.CompilerParams(
            collective_id=0, has_side_effects=True, vmem_limit_bytes=60 * 1024 * 1024
        ),
        name="contrastive",
    )(image, text)
    return loss.reshape(()), grad_scale * image_grad, grad_scale * text_grad


def solution(mesh):
    in_specs = (P(("row", "col"), None), P(("col", "row"), None))
    out_specs = (P(), P(("row", "col"), None), P(("col", "row"), None))
    return jax.shard_map(local, mesh=mesh, in_specs=in_specs, out_specs=out_specs, check_vma=False)
```

```python
import functools
import jax
import jax.numpy as jnp
from jax import lax
from jax.experimental import pallas as pl
from jax.experimental.pallas import tpu as pltpu
from jax.sharding import PartitionSpec as P

logit_scale = 20.0
grad_scale = 0.5 * logit_scale
MESH = pl.DeviceIdType.MESH
XN = 4
CORES = 2
H = 16
TREES = ((0, 0, 1, 2, 3), None, (0, 0, 1, 2, 3), (0, 0, 1, 2, 3))
MESSAGES = 76
ONE, TEXT, IMAGE, SUM1, SUM2, SUM3 = range(MESSAGES, MESSAGES + 6)
G = 4 * H
f32 = jnp.float32
bf16 = jnp.bfloat16
NT = (((1,), (1,)), ((), ()))
NN = (((1,), (0,)), ((), ()))
TN = (((0,), (0,)), ((), ()))


def dot3(a_hi, a_lo, b_hi, b_lo, dims):
    def dot(a, b):
        return lax.dot_general(a, b, dims, preferred_element_type=f32)

    return dot(a_hi, b_hi) + (dot(a_hi, b_lo) + dot(a_lo, b_hi))


def split(value):
    high = value.astype(bf16)
    return high, (value - high.astype(f32)).astype(bf16)


def merge(parts):
    peak = functools.reduce(jnp.maximum, [p for p, _ in parts])
    total = functools.reduce(jnp.add, [t * jnp.exp(p - peak) for p, t in parts])
    return peak, total


class Comm:
    def __init__(self, send_sem, recv_sem):
        self.send_sem, self.recv_sem, self.next = send_sem, recv_sem, 0

    def send(self, src, dst, device, group, shared=None):
        if shared is None:
            shared, self.next = self.next, self.next + 1
        copy = pltpu.make_async_remote_copy(
            src_ref=src,
            dst_ref=dst,
            send_sem=self.send_sem.at[group],
            recv_sem=self.recv_sem.at[shared],
            device_id=device,
            device_id_type=MESH,
        )
        copy.start()
        return copy

    def sent(self, group, like, device):
        pltpu.make_async_remote_copy(
            src_ref=like,
            dst_ref=like,
            send_sem=self.send_sem.at[group],
            recv_sem=self.recv_sem.at[0],
            device_id=device,
            device_id_type=MESH,
        ).wait_send()


    def received(self, shared, like, device):
        pltpu.make_async_remote_copy(
            src_ref=like,
            dst_ref=like,
            send_sem=self.send_sem.at[0],
            recv_sem=self.recv_sem.at[shared],
            device_id=device,
            device_id_type=MESH,
        ).wait_recv()


class Trees:
    def __init__(self, n):
        self.n, self.ahead, self.behind = n, n // 2, n - 1 - n // 2

    def parent(self, lo, d):
        return TREES[lo // H][d]

    def side(self, k):
        return (k, 1, self.ahead) if k <= self.ahead else (self.n - k, -1, self.behind)

    def sides(self, k):
        return [(0, 1, self.ahead), (0, -1, self.behind)] if k == 0 else [self.side(k)]

    def children(self, lo, d, most):
        return [c for c in range(most, d, -1) if self.parent(lo, c) == d]

    def slot(self, d, way):
        return (way * d) % self.n


class Gather(Trees):
    def __init__(self, comm, buf, n, ring, partner, other, group):
        super().__init__(n)
        self.comm, self.buf, self.at, self.partner, self.other, self.group = comm, buf, ring, partner, other, group
        self.cross, self.ring, self.core = {}, {}, {}

    def start(self):
        self.q_cross = self.comm.send(
            self.buf.at[0, 2 * H : 3 * H], self.buf.at[0, 3 * H : G], self.partner, self.group
        )
        self.forward(0, 0)
        self.send_cross(0)
        self.forward(0, 2 * H)

    def start_cross(self):
        self.q_cross.wait_recv()
        self.forward(0, 3 * H)

    def forward(self, k, lo):
        for d, way, most in self.sides(k):
            for c in self.children(lo, d, most):
                to = self.slot(c, way)
                self.ring[to, lo] = self.comm.send(
                    self.buf.at[k, lo : lo + H],
                    self.buf.at[to, lo : lo + H],
                    self.at((-way * (c - d)) % self.n),
                    self.group,
                )

    def send_cross(self, k):
        self.cross[k] = self.comm.send(
            self.buf.at[k, 0:H], self.buf.at[k, H : 2 * H], self.partner, self.group
        )

    def positions(self, s):
        if s > self.ahead:
            return []
        return sorted({s % self.n, (self.n - s) % self.n} if s <= self.behind else {s})

    def step(self, s, lo):
        for k in self.positions(s):
            self.ring[k, lo].wait_recv()
            self.forward(k, lo)
            if lo == 0:
                self.send_cross(k)

    def pass_core(self, k, lo):
        if self.other is not None:
            to = (self.n - k) % self.n
            self.core[to, lo] = self.comm.send(
                self.buf.at[k, lo : lo + 2 * H], self.buf.at[to, G + lo : G + lo + 2 * H], self.other, 1
            )

    def finish_q(self, s):
        for k in self.positions(s):
            self.pass_core(k, 2 * H)

    def finish_p(self, s):
        for k in self.positions(s):
            self.cross[k].wait_recv()
            self.pass_core(k, 0)


class Scatter(Trees):
    def __init__(self, comm, acc, cross_buf, up_buf, down_buf, q_cross, n, ring, partner, group):
        super().__init__(n)
        self.comm, self.acc, self.cross_buf = comm, acc, cross_buf
        self.bufs, self.q_cross_buf = {1: up_buf, -1: down_buf}, q_cross
        self.at, self.partner, self.group = ring, partner, group
        self.cross, self.rings = {}, {}
        self.far = sorted(range(n), key=lambda k: -min(k, n - k))

    def send_cross(self, k):
        self.cross[k] = self.comm.send(
            self.acc.at[k, H : 2 * H], self.cross_buf.at[k], self.partner, self.group
        )

    def leaf(self, k, lo):
        return not any(self.children(lo, d, most) for d, _, most in self.sides(k))

    def launch(self, k, lo):
        d, way, _ = self.side(k)
        dst = self.bufs[way].at[d - 1, lo : lo + H]
        to = self.at((way * (d - self.parent(lo, d))) % self.n)
        copy = self.comm.send(self.acc.at[k, lo : lo + H], dst, to, self.group)
        self.rings[way, d, lo] = (copy, dst)

    def begin(self, ks):
        for k in ks:
            self.send_cross(k)
        for k in ks:
            for lo in (3 * H, 2 * H):
                if self.leaf(k, lo):
                    self.launch(k, lo)

    def step(self, k, lo):
        if lo == 0:
            self.cross[k].wait_recv()
            self.acc[k, 0:H] += self.cross_buf[k]
            if self.leaf(k, lo):
                self.launch(k, lo)
        if self.leaf(k, lo):
            return
        for d, way, most in self.sides(k):
            for c in self.children(lo, d, most):
                copy, dst = self.rings[way, c, lo]
                copy.wait_recv()
                self.acc[k, lo : lo + H] += dst[...]
        if k:
            self.launch(k, lo)
        elif lo == 3 * H:
            self.last = self.comm.send(self.acc.at[0, lo:G], self.q_cross_buf, self.partner, self.group)

    def result(self, out):
        out[0:H] = self.acc[0, 0:H]
        self.last.wait_recv()
        out[H : 2 * H] = self.acc[0, 2 * H : 3 * H] + self.q_cross_buf[...]


def kernel(nz, ny, image, text, loss, image_grad, text_grad,
           T, I, Th, Tl, Ih, Il, L, Er, Ec, Wh, Wl, TP, CR, IP,
           tx, tu, td, tq, ix, iu, id_, iq,
           St, Si, R1t, R2t, R2i, Ft, Fi, L1, L2, L3, send_sem, recv_sem, own_sem):
    row, y = lax.axis_index("row"), lax.axis_index("col")
    x, z, c = row // (CORES * nz), (row // CORES) % nz, row % CORES
    turn = 1 - 2 * c
    xt = x + 1 - 2 * (x % 2)
    xi = XN - 1 - x

    def at(x_=x, y_=y, z_=z, c_=c):
        return (x_ * (CORES * nz) + z_ * CORES + c_, y_)

    z_of = [(z + turn * k + nz) % nz for k in range(nz)]
    y_of = [(y + turn * k + ny) % ny for k in range(ny)]
    z_ids, y_ids = [at(z_=v) for v in z_of], [at(y_=v) for v in y_of]
    ring_z, ring_y = z_ids.__getitem__, y_ids.__getitem__
    places = [(x * CORES + c + i) % (XN * CORES) for i in range(XN * CORES)]
    plane = [at(x_=j // CORES, c_=j % CORES) for j in places].__getitem__
    other, at_xt, at_xi = at(c_=1 - c), at(x_=xt), at(x_=xi)
    across_t, across_i = [at(x_=xt, z_=v) for v in z_of], [at(x_=xi, y_=v) for v in y_of]
    cols, rws = nz * 2 * G, ny * G
    comm = Comm(send_sem, recv_sem)

    own_copies = [
        pltpu.make_async_copy(src.at[h * H : (h + 1) * H], dst.at[0, 2 * h * H : (2 * h + 1) * H], own_sem.at[i, h])
        for i, (src, dst) in enumerate(((text, T), (image, I)))
        for h in (1, 0)
    ]
    for copy in own_copies:
        copy.start()
    barrier = pltpu.get_barrier_semaphore()
    peers = [ring_z(k) for k in range(1, nz)] + [ring_y(k) for k in range(1, ny)]
    peers += [plane(i) for i in range(1, XN * CORES)] + across_t[1:] + across_i[1:]
    for peer in peers:
        pl.semaphore_signal(barrier, inc=1, device_id=peer, device_id_type=MESH)
    for copy in own_copies:
        copy.wait()
    pl.semaphore_wait(barrier, len(peers))

    gt = Gather(comm, T, nz, ring_z, at_xt, other, 0)
    gi = Gather(comm, I, ny, ring_y, at_xi, None, 2)
    both = (gt, gi)
    for g in both:
        g.start()
    for g in both:
        g.start_cross()
    def late(s):
        for g in both:
            if s:
                g.step(s, 3 * H)
        for g in both:
            g.finish_q(s)
        for g in both:
            g.finish_p(s)

    last = max(nz, ny) // 2
    for s in range(1, last + 1):
        for lo in (0, 2 * H):
            for g in both:
                g.step(s, lo)
        late(s - 1)

    block = min(256, cols)
    blocks = cols // block
    per = block // 128
    half = ny // 2
    distance = lambda k, n: min(k, n - k)
    near_first = sorted(range(blocks), key=lambda b: max(distance(k, nz) for k in range(b * per, (b + 1) * per)))

    def take_image(h):
        for k in range(h * half, (h + 1) * half):
            Ih[k * G : (k + 1) * G], Il[k * G : (k + 1) * G] = split(I[k])

    def take_text(b):
        for k in range(b * per, (b + 1) * per):
            gt.core[k, 0].wait_recv()
            gt.core[k, 2 * H].wait_recv()
            first = k * 2 * G
            Th[first : first + 2 * G], Tl[first : first + 2 * G] = split(T[k])

    def logits(rows, b):
        span = slice(b * block, (b + 1) * block)
        L[rows, span] = logit_scale * dot3(Ih[rows], Il[rows], Th[span], Tl[span], NT)

    low, high = slice(0, half * G), slice(half * G, rws)
    take_image(0)
    for b in near_first[:-2]:
        take_text(b)
        logits(low, b)
    late(last)
    for b in near_first[:-1][-1:]:
        take_text(b)
        logits(low, b)
    take_image(1)
    for b in near_first[:-1]:
        logits(high, b)
    take_text(near_first[-1])
    logits(slice(0, rws), near_first[-1])

    def all_sent():
        comm.sent(0, T.at[0 : nz // 2, 0 : 2 * G - G // nz], other)
        comm.sent(1, T.at[0 : nz // 2], other)
        comm.sent(2, T.at[0 : ny // 2, 0 : 2 * G - G // ny], other)

    all_sent()
    def iota(shape, dim):
        return lax.broadcasted_iota(jnp.int32, shape, dim)

    lane = iota((1, cols), 1)
    at_z = (z + turn * (lane >> 7) + nz) & (nz - 1)
    at_x = jnp.where((lane >> 4) & 1 == 0, x, xt)
    at_c = jnp.where((lane >> 6) & 1 == 0, c, 1 - c)
    col_ids = (
        y * (XN * nz * CORES * 2 * H)
        + ((at_x * nz + at_z) * CORES + at_c) * (2 * H)
        + ((lane >> 5) & 1) * H
        + (lane & 15)
    )

    def row_ids(k):
        r = iota((G, 1), 0)
        of_x = jnp.where((r >> 4) & 1 == 0, x, xi)
        of_y = (y + turn * k + ny) & (ny - 1)
        return ((of_x * nz + z) * CORES + c) * (ny * 2 * H) + of_y * (2 * H) + ((r >> 5) & 1) * H + (r & 15)

    own_lane = iota((G, 128), 0) == iota((G, 128), 1)

    def to_lanes(column):
        return jnp.sum(jnp.where(own_lane, column, 0.0), axis=0, keepdims=True)

    def to_column(lanes):
        return jnp.sum(jnp.where(own_lane, lanes, 0.0), axis=1, keepdims=True)

    def group8(v, op):
        return op(v.reshape(v.shape[0] // 8, 8, v.shape[1]), axis=0)

    def share(buf, ids, n, group, shared):
        for p, ring in enumerate(ids):
            for k in range(1 - p, n):
                comm.send(buf.at[0], buf.at[p * n + (n - k) % n], ring[k], group, shared)

    def row_pass(k, diag):
        here = pl.ds(pl.multiple_of(k * G, G), G)
        tile = L[here]
        row_peak = jnp.max(tile, axis=1, keepdims=True)
        terms = jnp.exp(tile - row_peak)
        Er[here] = terms
        Si[0, pl.ds(k, 1)] = to_lanes(row_peak)
        Si[1, pl.ds(k, 1)] = to_lanes(jnp.sum(terms, axis=1, keepdims=True))
        return diag + group8(jnp.where(row_ids(k) == col_ids, tile, 0.0), jnp.sum)

    def peak_pass(k, peak):
        return jnp.maximum(peak, group8(L[pl.ds(pl.multiple_of(k * G, G), G)], jnp.max))

    peak8 = lax.fori_loop(0, ny, peak_pass, jnp.full((8, cols), -jnp.inf, f32))
    col_peak = jnp.max(peak8, axis=0, keepdims=True)

    def col_pass(k, total):
        here = pl.ds(pl.multiple_of(k * G, G), G)
        terms = jnp.exp(L[here] - col_peak)
        Ec[here] = terms
        return total + group8(terms, jnp.sum)

    col_total = jnp.sum(lax.fori_loop(0, ny, col_pass, jnp.zeros((8, cols), f32)), axis=0, keepdims=True)

    def fold(v):
        return jnp.concatenate([v[:, k * 128 : (k + 1) * 128] for k in range(nz)], axis=0)

    St[0], St[1] = fold(col_peak), fold(col_total)
    comm.send(St, R1t, other, 3, ONE)
    diag8 = lax.fori_loop(0, ny, row_pass, jnp.zeros((8, cols), f32))
    valid = iota((ny, 128), 1) < G
    R2i[0] = jnp.where(valid, Si[0], pltpu.roll(Si[1], G, 1))
    share(R2i, [y_ids, across_i], ny, 8, IMAGE)
    lanes_n = cols // 128
    diag_sum = functools.reduce(jnp.add, [diag8[:, i * 128 : (i + 1) * 128] for i in range(lanes_n)])


    def swap_x(v):
        low = (iota(v.shape, 1) >> 4) & 1 == 0
        return jnp.where(low, pltpu.roll(v, 128 - H, 1), pltpu.roll(v, H, 1))

    def swap_core(v):
        v = pltpu.roll(v, G, 1)
        return jnp.concatenate([v[(nz - k) % nz : (nz - k) % nz + 1] for k in range(nz)], axis=0)

    def shift(v, k, n):
        return jnp.concatenate([v[n - k :], v[: n - k]], axis=0)

    def ring_of(buf, n):
        for p in range(2):
            for k in range(n):
                v = swap_x(buf[p * n + k]) if p else buf[k]
                yield shift(v, k, n) if k else v

    peak_t, peak_i = St[0], Si[0]
    comm.received(ONE, R1t, other)
    pt, tt = merge([(peak_t, St[1]), (swap_core(R1t[0]), swap_core(R1t[1]))])
    R2t[0] = pt + jnp.log(tt)
    share(R2t, [z_ids, across_t], nz, 7, TEXT)
    comm.received(IMAGE, R2i.at[1:], other)
    pi, ti = merge([
        (jnp.where(valid, v, 0.0), jnp.where(valid, pltpu.roll(v, G, 1), 1.0)) for v in ring_of(R2i, ny)
    ])
    comm.received(TEXT, R2t.at[1:], other)
    pt, tt = merge([(v, 1.0) for v in ring_of(R2t, nz)])
    Ft[...] = jnp.exp(peak_t - pt) / tt
    Fi[...] = jnp.exp(peak_i - pi) / ti

    def own(v):
        i = iota(v.shape, 1)
        mine = (iota(v.shape, 0) == 0) & (i < G) & ((i >> 4) & 1 == 0)
        return jnp.sum(jnp.where(mine, v, 0.0), axis=0, keepdims=True)

    first = iota((8, 128), 0) == 0
    part = own(pt + jnp.log(tt)) + own(pi + jnp.log(ti))
    L1[x * CORES + c] = jnp.where(first, part, 0.0) - 2.0 * diag_sum
    for i in range(1, XN * CORES):
        comm.send(L1.at[x * CORES + c], L1.at[x * CORES + c], plane(i), 4, SUM1)

    col_factor = jnp.concatenate([Ft[k : k + 1] for k in range(nz)], axis=1)

    def weigh(k, _):
        here = pl.ds(pl.multiple_of(k * G, G), G)
        value = Er[here] * to_column(Fi[pl.ds(k, 1)]) + Ec[here] * col_factor
        value = value - jnp.where(row_ids(k) == col_ids, 2.0, 0.0)
        Wh[here], Wl[here] = split(value)
        return 0

    lax.fori_loop(0, ny, weigh, 0)

    comm.next = 0
    st = Scatter(comm, TP, tx, tu, td, tq, nz, ring_z, at_xt, 0)
    si = Scatter(comm, IP, ix, iu, id_, iq, ny, ring_y, at_xi, 2)
    core, done, added, pending = {}, [], [], []

    def add_core():
        for k in pending:
            core[k].wait_recv()
            TP[k, 0:G] += CR[k]
        st.begin(pending)
        added.extend(pending)
        pending.clear()

    def gradients(b, image_positions):
        span = slice(b * block, (b + 1) * block)
        part = dot3(Wh[:, span], Wl[:, span], Ih[...], Il[...], TN)
        here = list(range(b * per, (b + 1) * per))
        for i, k in enumerate(here):
            TP[k] = part[i * 128 : (i + 1) * 128]
            to = (nz - k) % nz
            core[to] = comm.send(TP.at[k, G : 2 * G], CR.at[to], other, 1)
        add_core()
        if image_positions:
            rows = slice(image_positions[0] * G, (image_positions[-1] + 1) * G)
            part = dot3(Wh[rows], Wl[rows], Th[...], Tl[...], NN)
            for i, k in enumerate(image_positions):
                IP[k] = part[i * G : (i + 1) * G]
            si.begin([k for k in si.far if k in image_positions])
        done.extend(here)
        pending.extend(k for k in st.far if k in done and (nz - k) % nz in done and k not in added)

    steps = [(d, lo) for d in range(nz // 2, -1, -1) for lo in (3 * H, 2 * H, 0)]

    def run(some):
        for d, lo in some:
            for sc in (si, st):
                for k in sorted({d, (nz - d) % nz}):
                    if k <= sc.ahead or d <= sc.behind:
                        sc.step(k, lo)

    early = 5 if blocks > 2 else 0
    shares = {0: range(half, ny), max(blocks - 3, 1): range(half)} if blocks > 1 else {0: range(ny)}
    for i, b in enumerate(near_first[:0:-1]):
        gradients(b, shares.get(i))
    run(steps[:early])
    comm.received(SUM1, L1.at[1:], other)
    L2[y] = functools.reduce(jnp.add, [L1[i] for i in range(XN * CORES)])
    for k in range(1, ny):
        comm.send(L2.at[y], L2.at[y], ring_y(k), 5, SUM2)
    gradients(near_first[0], shares.get(blocks - 1))
    run(steps[early : early + 1])
    add_core()
    run(steps[early + 1 : early + 3])
    comm.received(SUM2, L2.at[1:], other)
    L3[z] = functools.reduce(jnp.add, [L2[i] for i in range(ny)])
    for k in range(1, nz):
        comm.send(L3.at[z], L3.at[z], ring_z(k), 6, SUM3)
    run(steps[early + 3 : -1])
    comm.received(SUM3, L3.at[1:], other)
    samples = XN * nz * CORES * ny * 2 * H
    loss[0, 0] = jnp.sum(functools.reduce(jnp.add, [L3[i] for i in range(nz)])) / (2.0 * samples)
    run(steps[-1:])
    si.result(image_grad)
    st.result(text_grad)
    all_sent()
    comm.sent(3, R1t, other)
    comm.sent(7, R2t.at[1:], other)
    comm.sent(8, R2i.at[1:], other)
    comm.sent(4, L1.at[1:], other)
    comm.sent(5, L2.at[1:], other)
    comm.sent(6, L3.at[1:], other)


def local(image, text):
    nz = lax.axis_size("row") // (XN * CORES)
    ny = lax.axis_size("col")
    E = image.shape[1]
    cols, rws = nz * 2 * G, ny * G
    vmem = lambda *shape, dtype=f32: pltpu.VMEM(shape, dtype)

    def ring(n):
        ahead, behind = n // 2, max(n - 1 - n // 2, 1)
        return [vmem(n, H, E), vmem(ahead, G, E), vmem(behind, G, E), vmem(H, E)]

    scratch = [
        vmem(nz, 2 * G, E),
        vmem(ny, G, E),
        vmem(cols, E, dtype=bf16),
        vmem(cols, E, dtype=bf16),
        vmem(rws, E, dtype=bf16),
        vmem(rws, E, dtype=bf16),
        vmem(rws, cols),
        vmem(rws, cols),
        vmem(rws, cols),
        vmem(rws, cols, dtype=bf16),
        vmem(rws, cols, dtype=bf16),
        vmem(nz, 2 * G, E),
        vmem(nz, G, E),
        vmem(ny, G, E),
        *ring(nz),
        *ring(ny),
        vmem(2, nz, 128),
        vmem(2, ny, 128),
        vmem(2, nz, 128),
        vmem(2 * nz, nz, 128),
        vmem(2 * ny, ny, 128),
        vmem(nz, 128),
        vmem(ny, 128),
        vmem(XN * CORES, 8, 128),
        vmem(ny, 8, 128),
        vmem(nz, 8, 128),
        pltpu.SemaphoreType.DMA((9,)),
        pltpu.SemaphoreType.DMA((MESSAGES + 6,)),
        pltpu.SemaphoreType.DMA((2, 2)),
    ]
    block = pl.BlockSpec(memory_space=pltpu.VMEM)
    loss, image_grad, text_grad = pl.pallas_call(
        functools.partial(kernel, nz, ny),
        out_shape=(
            jax.ShapeDtypeStruct((1, 1), f32),
            jax.ShapeDtypeStruct(image.shape, f32),
            jax.ShapeDtypeStruct(text.shape, f32),
        ),
        in_specs=[pl.BlockSpec(memory_space=pltpu.HBM)] * 2,
        out_specs=(pl.BlockSpec(memory_space=pltpu.SMEM), block, block),
        scratch_shapes=scratch,
        compiler_params=pltpu.CompilerParams(
            collective_id=0, has_side_effects=True, vmem_limit_bytes=60 * 1024 * 1024
        ),
        name="contrastive",
    )(image, text)
    return loss.reshape(()), grad_scale * image_grad, grad_scale * text_grad


def solution(mesh):
    in_specs = (P(("row", "col"), None), P(("col", "row"), None))
    out_specs = (P(), P(("row", "col"), None), P(("col", "row"), None))
    return jax.shard_map(local, mesh=mesh, in_specs=in_specs, out_specs=out_specs, check_vma=False)
```
